512 devices in a mesh: lat: 64 (over z_hi, x, y, core), lev: 8 (over z_lo).
Axes of the slice: x: 4, y: 4, z: 16 (z_hi: 2, z_lo: 8; z = z_hi * 8 + z_lo), core: 2. Of those that a mesh axis runs over, the one named last changes fastest.
Arguments:
- level_tokens: bfloat16 [64, 512, 40, 512], P('lat', None, 'lev'), may hold values from -6 to 6
- latent_queries: bfloat16 [4, 512], replicated, may hold values from -1200 to 1200
- key_weight: bfloat16 [512, 512], replicated, may hold values from -0.25 to 0.25
- value_weight: bfloat16 [512, 512], replicated, may hold values from -0.25 to 0.25
- out_weight: bfloat16 [512, 512], replicated, may hold values from -0.25 to 0.25
- level_valid: int32 [40], replicated, may hold values from 0 to 1, as said below
- pole_partner: int32 [512], P('lev'), may hold values from 0 to 511, as said below
Outputs:
- diffused: bfloat16 [64, 512, 2048], P('lat', 'lev')
The draws below stay inside these ranges and needn't reach their ends.
Inputs may be any that keep to these rules, and one draw needn't show every extreme that they name: `level_valid`: each aligned group of 5 levels holds at least one valid level. pole_partner[c] lies in the sector of 64 longitudes that is half the sectors away: pole_partner[c] // 64 == (c // 64 + 512 // 128) % 8; within each sector the map is a permutation.
All inputs are finite; a program needn't handle non-finite values.
Results may differ from the reference program's by a relative error of at most 0.013.
The reference program's roundings to bfloat16 on the way (of `pooled`) count: a program that leaves them out, or rounds other values in their place, can miss the bound.
Values may be sent and summed in bfloat16 or wider, within the bound.
No kernel may reach another device: no remote copies, remote signals or barrier semaphores. Data moves between devices by JAX's collectives and lax.ppermute only.
A program may use at most 128 MiB of HBM per device.

```python
import math
import jax
import jax.numpy as jnp
from jax import lax

E = 512
HEADS = 8
LATENTS = 4
LEV_DEV = 5
HOPS = 3
SEC = 64
LEVELS = 40
NLAT = 64
NLON = 512


def draw_latent_queries(key, part):
    key = jax.random.fold_in(key, 11)
    base_key = jax.random.fold_in(key, 0)
    base = jnp.clip(jax.random.normal(base_key, (LATENTS, E), jnp.float32), -4.0, 4.0)
    return base.astype(jnp.bfloat16)


def draw_level_valid(key, part):
    key = jax.random.fold_in(key, 12)
    first_key, second_key = jax.random.split(key)
    groups = LEVELS // LEV_DEV
    valid = (jax.random.randint(first_key, (LEVELS,), 0, 4) > 0).astype(jnp.int32)
    chosen = jax.random.randint(second_key, (groups,), 0, LEV_DEV)
    places = jnp.arange(groups, dtype=jnp.int32) * LEV_DEV + chosen
    return valid.at[places].set(1)


def draw_pole_partner(key, part):
    key = jax.random.fold_in(key, 13)
    groups = NLON // SEC
    sectors = jnp.arange(groups, dtype=jnp.int32)

    def one_sector(index):
        order = jax.random.permutation(jax.random.fold_in(key, index), SEC).astype(jnp.int32)
        return (index + groups // 2) % groups * SEC + order
    return jax.vmap(one_sector)(sectors).reshape(NLON).astype(jnp.int32)


def shard_levels(own_key, dims, pieces, low, high):
    def one(position, shards_of):
        heights = jax.random.uniform(jax.random.fold_in(jax.random.fold_in(own_key, 6), position), (shards_of,), jnp.float32, low / len(pieces), high / len(pieces))
        return jnp.repeat(jnp.exp(heights), dims[position] // shards_of).reshape((-1,) + (1,) * (len(dims) - position - 1))

    level = one(*pieces[0])
    for cut in pieces[1:]:
        level = level * one(*cut)
    return level


def scatter_about(own_key, extent, deviation, most, cuts=(), held_as=jnp.bfloat16):
    result = deviation * jax.random.normal(own_key, extent, jnp.float32)
    if cuts:
        result = result * shard_levels(own_key, extent, cuts, -0.22, 0.18)
    return jnp.clip(result, -most, most).astype(held_as)


def setup_inputs(seed: int = 0) -> dict:
    key_list = jax.random.split(jax.random.key(seed), 8)
    level_tokens = scatter_about(key_list[0], (NLAT, NLON, LEVELS, E), 1.0, 6.0, ((0, 64), (2, 8)))
    latent_queries = draw_latent_queries(jax.random.fold_in(key_list[7], 71), 0)
    key_weight = scatter_about(key_list[2], (E, E), E ** -0.5, 0.25)
    value_weight = scatter_about(key_list[3], (E, E), E ** -0.5, 0.25)
    out_weight = scatter_about(key_list[4], (E, E), E ** -0.5, 0.25)
    level_valid = draw_level_valid(jax.random.fold_in(key_list[7], 71), 0)
    pole_partner = draw_pole_partner(jax.random.fold_in(key_list[7], 71), 0)
    return {"level_tokens": level_tokens, "latent_queries": latent_queries, "key_weight": key_weight, "value_weight": value_weight, "out_weight": out_weight, "level_valid": level_valid, "pole_partner": pole_partner}


def pool_row(row, latent_queries, key_weight, value_weight, out_weight, level_valid):
    head = E // HEADS
    flat = row.reshape(-1, E)
    keys = jnp.dot(flat, key_weight, preferred_element_type=jnp.float32).astype(jnp.bfloat16)
    values = jnp.dot(flat, value_weight, preferred_element_type=jnp.float32).astype(jnp.bfloat16)
    keys = keys.astype(jnp.float32).reshape(NLON, LEVELS, HEADS, head)
    values = values.astype(jnp.float32).reshape(NLON, LEVELS, HEADS, head)
    query = latent_queries.astype(jnp.float32).reshape(LATENTS, HEADS, head)
    scores = jnp.einsum('clhd,khd->clkh', keys, query) / math.sqrt(head)
    keep = (level_valid == 1)[None, :, None, None]
    masked = jnp.where(keep, scores, -1e+30)
    top = lax.optimization_barrier(jnp.max(masked, axis=1, keepdims=True))
    expo = jnp.where(keep, jnp.exp(masked - top), 0.0)
    weights = expo / lax.optimization_barrier(jnp.sum(expo, axis=1, keepdims=True))
    pooled = jnp.einsum('clkh,clhd->ckhd', weights, values).astype(jnp.bfloat16)
    state = jnp.dot(pooled.reshape(-1, E), out_weight, preferred_element_type=jnp.float32)
    return state.reshape(NLON, LATENTS * E)

def area_of(rows):
    angle = math.pi * (rows.astype(jnp.float32) + 0.5) / NLAT - math.pi / 2
    return jnp.cos(angle)

def reference(level_tokens, latent_queries, key_weight, value_weight, out_weight, level_valid, pole_partner):
    state = lax.map(lambda row: pool_row(row, latent_queries, key_weight, value_weight, out_weight, level_valid), level_tokens)
    rows = jnp.arange(NLAT, dtype=jnp.int32)
    area = area_of(rows)[:, None, None]
    north_area = area_of(jnp.maximum(rows - 1, 0))[:, None, None]
    south_area = area_of(jnp.minimum(rows + 1, NLAT - 1))[:, None, None]
    denom = 3.0 * area + north_area + south_area
    total = state
    for step in range(HOPS):
        first = jnp.take(state[0], pole_partner, axis=0)[None]
        last = jnp.take(state[NLAT - 1], pole_partner, axis=0)[None]
        north = jnp.concatenate([first, state[:-1]], axis=0)
        south = jnp.concatenate([state[1:], last], axis=0)
        east = jnp.roll(state, -1, axis=1)
        west = jnp.roll(state, 1, axis=1)
        state = (area * (state + east + west) + north_area * north + south_area * south) / denom
        total = total + state
    return (total / (HOPS + 1.0)).astype(jnp.bfloat16)
```

```python
import functools
import math

import jax
import jax.numpy as jnp
import numpy as np
from jax import lax
from jax.experimental import pallas as pl
from jax.experimental.pallas import tpu as pltpu
from jax.sharding import Mesh
from jax.sharding import PartitionSpec as P

HEADS = 8
LATENTS = 4
HOPS = 3
E = 512
HEAD = E // HEADS
NLAT = 64
NLON = 512
LEV = 8
SEC = NLON // LEV
LEV_DEV = 5
GROUP = 32
FEATS = LATENTS * E // LEV
COMBOS = FEATS // HEAD
CHUNKS = 2
CELLS = NLON // CHUNKS
ROWS = FEATS + 16
RING = (0, 2, 4, 6, 7, 5, 3, 1)
F32 = jnp.float32
BF16 = jnp.bfloat16
NT = (((1,), (1,)), ((), ()))
VMEM_LIMIT = 48 * 1024 * 1024


def pieces(x):
    high = x.astype(BF16).astype(F32)
    rest = x - high
    mid = rest.astype(BF16).astype(F32)
    return high, mid, rest - mid


def stat_rows(lse, partner):
    high, mid, low = pieces(lse)
    empty = jnp.zeros((16 - 3 * COMBOS - 1, lse.shape[1]), F32)
    return jnp.concatenate([high, mid, low, partner, empty], axis=0).astype(BF16)


def level_kernel(
    meta, valid, query, key_weight, value_weight, tokens, partner, out, first, values, weights
):
    lev = meta[LEV]
    lane_head = lax.broadcasted_iota(jnp.int32, (HEADS, E), 1) // HEAD
    own_head = lane_head == lax.broadcasted_iota(jnp.int32, (HEADS, E), 0)
    spread = [
        jnp.where(own_head, query[pl.ds(k, 1), :].astype(F32), 0.0) for k in range(LATENTS)
    ]
    spread = jnp.concatenate(spread, axis=0).astype(BF16)
    value_t = value_weight[...].astype(F32).T.astype(BF16)
    scores = []
    for level in range(LEV_DEV):
        block = tokens[level]
        keys = jnp.dot(block, key_weight[...], preferred_element_type=F32).astype(BF16)
        score = lax.dot_general(spread, keys, NT, preferred_element_type=F32)
        score = score * (1.0 / math.sqrt(HEAD))
        scores.append(jnp.where(valid[lev * LEV_DEV + level] == 1, score, -1e30))
        value = lax.dot_general(value_t, block, NT, preferred_element_type=F32)
        values[level] = value.astype(BF16).astype(F32)
    top = functools.reduce(jnp.maximum, scores)
    expo = []
    for level in range(LEV_DEV):
        kept = valid[lev * LEV_DEV + level] == 1
        expo.append(jnp.where(kept, jnp.exp(scores[level] - top), 0.0))
    total = functools.reduce(jnp.add, expo)
    for level in range(LEV_DEV):
        weights[level] = expo[level] / total
    lse = top + jnp.log(total)
    for head in range(HEADS):
        for lane in range(0, CELLS, 128):
            lanes = pl.ds(lane, 128)
            terms = [
                values[level, pl.ds(head * HEAD, HEAD), lanes] for level in range(LEV_DEV)
            ]
            for latent in range(LATENTS):
                row = pl.ds(latent * HEADS + head, 1)
                summed = weights[0, row, lanes] * terms[0]
                for level in range(1, LEV_DEV):
                    summed = summed + weights[level, row, lanes] * terms[level]
                block, place = divmod(latent * HEADS + head, COMBOS)
                out[block, pl.ds(place * HEAD, HEAD), lanes] = summed.astype(BF16)
    for block in range(LEV):
        out[block, pl.ds(FEATS, 16), :] = stat_rows(
            lse[block * COMBOS : (block + 1) * COMBOS], partner[...]
        )
    first[...] = out[meta[0]]


def level_terms(chunk, meta, valid, query, key_weight, value_weight, tokens, partner):
    whole = pl.BlockSpec((E, E), lambda i: (0, 0))
    smem = pl.BlockSpec(memory_space=pltpu.SMEM)
    return pl.pallas_call(
        level_kernel,
        grid=(1,),
        out_shape=(
            jax.ShapeDtypeStruct((LEV, ROWS, CELLS), BF16),
            jax.ShapeDtypeStruct((ROWS, CELLS), BF16),
        ),
        in_specs=[
            smem,
            smem,
            pl.BlockSpec((LATENTS, E), lambda i: (0, 0)),
            whole,
            whole,
            pl.BlockSpec((LEV_DEV, CELLS, E), lambda i: (0, chunk, 0)),
            pl.BlockSpec((1, CELLS), lambda i: (0, chunk)),
        ],
        out_specs=(
            pl.BlockSpec((LEV, ROWS, CELLS), lambda i: (0, 0, 0)),
            pl.BlockSpec((ROWS, CELLS), lambda i: (0, 0)),
        ),
        scratch_shapes=[
            pltpu.VMEM((LEV_DEV, E, CELLS), F32),
            pltpu.VMEM((LEV_DEV, LATENTS * HEADS, CELLS), F32),
        ],
        compiler_params=pltpu.CompilerParams(vmem_limit_bytes=VMEM_LIMIT),
        name="level_terms",
    )(meta, valid, query, key_weight, value_weight, tokens, partner)


def merged(came, own, own_at=()):
    stats = came[pl.ds(FEATS, 16), :].astype(F32)
    mine = own[(*own_at, pl.ds(FEATS, 16), slice(None))].astype(F32)
    n = COMBOS
    there = stats[0:n] + stats[n : 2 * n] + stats[2 * n : 3 * n]
    here = mine[0:n] + mine[n : 2 * n] + mine[2 * n : 3 * n]
    best = jnp.maximum(there, here)
    grow = jnp.exp(there - best)
    total = grow + jnp.exp(here - best)
    share = grow / total
    partner = stats[3 * n : 3 * n + 1] + mine[3 * n : 3 * n + 1]
    blocks = []
    for place in range(COMBOS):
        rows = pl.ds(place * HEAD, HEAD)
        far = came[rows, :].astype(F32)
        near = own[(*own_at, rows, slice(None))].astype(F32)
        blocks.append(near + share[place : place + 1] * (far - near))
    return blocks, best + jnp.log(total), partner


def hop_kernel(meta, came, own, out):
    blocks, lse, partner = merged(came, own, (0,))
    for place in range(COMBOS):
        out[pl.ds(place * HEAD, HEAD), :] = blocks[place].astype(BF16)
    out[pl.ds(FEATS, 16), :] = stat_rows(lse, partner)


def hop(step, meta, came, own):
    return pl.pallas_call(
        hop_kernel,
        out_shape=jax.ShapeDtypeStruct((ROWS, CELLS), BF16),
        grid_spec=pltpu.PrefetchScalarGridSpec(
            num_scalar_prefetch=1,
            grid=(1,),
            in_specs=[
                pl.BlockSpec((ROWS, CELLS), lambda i, meta: (0, 0)),
                pl.BlockSpec((1, ROWS, CELLS), lambda i, meta: (meta[step], 0, 0)),
            ],
            out_specs=pl.BlockSpec((ROWS, CELLS), lambda i, meta: (0, 0)),
        ),
        name="hop",
    )(meta, came, own)


def last_kernel(meta, *refs):
    came, own, (out, across) = refs[:CHUNKS], refs[CHUNKS : 2 * CHUNKS], refs[2 * CHUNKS :]
    for chunk in range(CHUNKS):
        blocks, _, partner = merged(came[chunk], own[chunk], (0,))
        lanes = pl.ds(chunk * CELLS, CELLS)
        for place in range(COMBOS):
            out[pl.ds(place * HEAD, HEAD), lanes] = blocks[place].astype(BF16)
        across[:, lanes] = jnp.broadcast_to(partner, (8, CELLS))


def last_hop(meta, came, own):
    return pl.pallas_call(
        last_kernel,
        out_shape=(
            jax.ShapeDtypeStruct((FEATS, NLON), BF16),
            jax.ShapeDtypeStruct((8, NLON), F32),
        ),
        grid_spec=pltpu.PrefetchScalarGridSpec(
            num_scalar_prefetch=1,
            grid=(1,),
            in_specs=[pl.BlockSpec((ROWS, CELLS), lambda i, meta: (0, 0))] * CHUNKS
            + [pl.BlockSpec((1, ROWS, CELLS), lambda i, meta: (meta[LEV - 1], 0, 0))] * CHUNKS,
            out_specs=(
                pl.BlockSpec((FEATS, NLON), lambda i, meta: (0, 0)),
                pl.BlockSpec((8, NLON), lambda i, meta: (0, 0)),
            ),
        ),
        name="last_hop",
    )(meta, *came, *own)


def pole_kernel(across, out):
    lane = lax.broadcasted_iota(jnp.int32, (1, NLON), 1)
    sector = (lane // SEC + LEV // 2) % LEV
    source = sector * SEC + across[0:1, :].astype(jnp.int32)
    place = lax.broadcasted_iota(jnp.int32, (NLON, NLON), 0)
    out[...] = jnp.where(place == source, 1.0, 0.0).astype(BF16)


def area_of(row):
    return math.cos(math.pi * (row + 0.5) / NLAT - math.pi / 2)


def coefficients(row):
    area, polar, inner = area_of(row), area_of(max(row - 1, 0)), area_of(row + 1)
    denom = 3.0 * area + polar + inner
    return area / denom, polar / denom, inner / denom


def diffuse_kernel(meta, rows, halo, pole, out, raw, edge, one, two):
    south = meta[LEV + 1]
    raw[...] = rows[...].astype(F32)
    edge[...] = halo[...].astype(F32)

    def start(row):
        if row < GROUP:
            return raw[row + south * (GROUP - 1 - 2 * row)]
        k = row - GROUP
        return edge[k + south * (HOPS - 1 - 2 * k)]

    readers = (start, lambda row: one[row], lambda row: two[row])
    for step in range(HOPS):
        read = readers[step]
        here = read(0)
        high, mid, _ = pieces(here)
        both = jnp.concatenate([high, mid], axis=0).astype(BF16)
        turned = jnp.dot(both, pole[...], preferred_element_type=F32)
        before = turned[0:8] + turned[8:16]
        for row in range(GROUP + HOPS - 1 - step):
            after = read(row + 1)
            area, polar, inner = coefficients(row)
            beside = pltpu.roll(here, 1, 1) + pltpu.roll(here, NLON - 1, 1)
            state = area * (here + beside) + polar * before + inner * after
            if step == 0:
                one[row] = state
            elif step == 1:
                two[row] = state
            else:
                total = start(row) + one[row] + here + state
                raw[row + south * (GROUP - 1 - 2 * row)] = total * (1.0 / (HOPS + 1.0))
            before, here = here, after
    out[...] = raw[...].astype(BF16)


def diffuse(meta, rows, halo, pole):
    smem = pl.BlockSpec(memory_space=pltpu.SMEM)
    vmem = pl.BlockSpec(memory_space=pltpu.VMEM)
    return pl.pallas_call(
        diffuse_kernel,
        out_shape=jax.ShapeDtypeStruct(rows.shape, BF16),
        in_specs=[smem, vmem, vmem, vmem],
        out_specs=vmem,
        scratch_shapes=[
            pltpu.VMEM((GROUP, 8, NLON), F32),
            pltpu.VMEM((HOPS, 8, NLON), F32),
            pltpu.VMEM((GROUP + HOPS, 8, NLON), F32),
            pltpu.VMEM((GROUP + HOPS, 8, NLON), F32),
        ],
        compiler_params=pltpu.CompilerParams(vmem_limit_bytes=VMEM_LIMIT),
        name="diffuse",
    )(meta, rows, halo, pole)


def project_kernel(parts, weight, out):
    for latent in range(LATENTS):
        summed = jnp.dot(parts[2 * latent], weight[0:FEATS], preferred_element_type=F32)
        summed += jnp.dot(parts[2 * latent + 1], weight[FEATS:E], preferred_element_type=F32)
        out[0, :, pl.ds(latent * E, E)] = summed.astype(BF16)


def whole_call(kernel, shape, dtype, name, *args):
    vmem = pl.BlockSpec(memory_space=pltpu.VMEM)
    return pl.pallas_call(
        kernel,
        out_shape=jax.ShapeDtypeStruct(shape, dtype),
        in_specs=[vmem] * len(args),
        out_specs=vmem,
        compiler_params=pltpu.CompilerParams(vmem_limit_bytes=VMEM_LIMIT),
        name=name,
    )(*args)


def body(
    level_tokens, latent_queries, key_weight, value_weight, out_weight, level_valid, pole_partner
):
    lev = lax.axis_index("lev")
    south = lax.axis_index("half")
    table = np.zeros((LEV, LEV), np.int32)
    for place, index in enumerate(RING):
        for step in range(LEV):
            table[index, step] = RING[(place - 1 - step) % LEV]
    order = lax.dynamic_index_in_dim(jnp.asarray(table), lev, 0, False)
    meta = jnp.concatenate([order, jnp.stack([lev, south]).astype(jnp.int32)])
    local = jnp.tile((pole_partner % SEC).astype(F32), LEV)
    sector = jnp.arange(NLON, dtype=jnp.int32) // SEC
    partner = jnp.where(sector == lev, local, 0.0)[None]
    tokens = jnp.transpose(level_tokens[0], (1, 0, 2))

    ring = [(RING[i], RING[(i + 1) % LEV]) for i in range(LEV)]
    own, going = [], []
    for chunk in range(CHUNKS):
        terms, first = level_terms(
            chunk, meta, level_valid, latent_queries, key_weight, value_weight, tokens, partner
        )
        own.append(terms)
        going.append(first)
    for step in range(LEV - 1):
        came = [lax.ppermute(message, "lev", ring) for message in going]
        if step < LEV - 2:
            going = [hop(step + 1, meta, came[c], own[c]) for c in range(CHUNKS)]
    pooled, across = last_hop(meta, came, own)

    rows = pooled.reshape(GROUP, FEATS // GROUP, NLON)
    rows = lax.all_to_all(rows, "row", split_axis=0, concat_axis=0, tiled=True)
    edge = jnp.where(south == 1, rows[:HOPS], rows[GROUP - HOPS :])
    halo = lax.ppermute(edge, "half", [(0, 1), (1, 0)])
    pole = whole_call(pole_kernel, (NLON, NLON), BF16, "pole", across)
    mean = diffuse(meta, rows, halo, pole)
    mean = lax.all_to_all(mean, "row", split_axis=0, concat_axis=0, tiled=True)
    sectors = mean.reshape(FEATS, NLON).T.reshape(LEV, SEC, FEATS)
    parts = lax.all_to_all(sectors, "lev", split_axis=0, concat_axis=0, tiled=True)
    return whole_call(
        project_kernel, (1, SEC, LATENTS * E), BF16, "project", parts, out_weight
    )


def solution(mesh):
    halves = mesh.shape["lat"] // GROUP
    devices = mesh.devices.reshape(halves, GROUP, mesh.shape["lev"])
    mesh = Mesh(devices, ("half", "row", "lev"))
    lat = ("half", "row")
    in_specs = (P(lat, None, "lev", None), P(), P(), P(), P(), P(), P("lev"))
    out_specs = P(lat, "lev", None)
    return jax.shard_map(body, mesh=mesh, in_specs=in_specs, out_specs=out_specs, check_vma=False)
```

```python
import functools
import math

import jax
import jax.numpy as jnp
from jax import lax
from jax.experimental import pallas as pl
from jax.experimental.pallas import tpu as pltpu
from jax.sharding import Mesh
from jax.sharding import PartitionSpec as P

HEADS = 8
LATENTS = 4
HOPS = 3
E = 512
HEAD = E // HEADS
NLAT = 64
NLON = 512
LEV = 8
SEC = NLON // LEV
LEV_DEV = 5
GROUP = 32
FEATS = LATENTS * E // LEV
COMBOS = FEATS // HEAD
CHUNKS = 2
CELLS = NLON // CHUNKS
ROWS = FEATS + 16
RING = (0, 2, 4, 6, 7, 5, 3, 1)
F32 = jnp.float32
BF16 = jnp.bfloat16
NT = (((1,), (1,)), ((), ()))
VMEM_LIMIT = 8 * 1024 * 1024
LEVEL_LIMIT = 16 * 1024 * 1024


def pieces(x):
    high = x.astype(BF16).astype(F32)
    rest = x - high
    mid = rest.astype(BF16).astype(F32)
    return high, mid, rest - mid


def stat_rows(lse, partner):
    high, mid, low = pieces(lse)
    empty = jnp.zeros((16 - 3 * COMBOS - 1, lse.shape[1]), F32)
    return jnp.concatenate([high, mid, low, partner, empty], axis=0).astype(BF16)


def level_kernel(
    chunk, valid_at, query_at, key_at, value_at, tokens_at, partner_at,
    own, first, values, weights, valid, query, key_weight, value_weight, tokens, partner, sems,
):
    lev = lax.axis_index("lev")
    cells = pl.ds(chunk * CELLS, CELLS)
    copies = [
        pltpu.make_async_copy(key_at, key_weight, sems.at[0]),
        pltpu.make_async_copy(query_at, query, sems.at[1]),
        pltpu.make_async_copy(valid_at, valid, sems.at[2]),
        pltpu.make_async_copy(value_at, value_weight, sems.at[3]),
        pltpu.make_async_copy(partner_at, partner, sems.at[4]),
    ]
    fetches = [
        pltpu.make_async_copy(tokens_at.at[level, cells], tokens.at[level], sems.at[5 + level])
        for level in range(LEV_DEV)
    ]
    for copy in copies[:4] + fetches + copies[4:]:
        copy.start()
    for copy in copies[:4]:
        copy.wait()
    lane_head = lax.broadcasted_iota(jnp.int32, (HEADS, E), 1) // HEAD
    own_head = lane_head == lax.broadcasted_iota(jnp.int32, (HEADS, E), 0)
    spread = [
        jnp.where(own_head, query[pl.ds(k, 1), :].astype(F32), 0.0) for k in range(LATENTS)
    ]
    spread = jnp.concatenate(spread, axis=0).astype(BF16)
    value_t = value_weight[...].astype(F32).T.astype(BF16)
    scores = []
    for level in range(LEV_DEV):
        fetches[level].wait()
        block = tokens[level]
        keys = jnp.dot(block, key_weight[...], preferred_element_type=F32).astype(BF16)
        score = lax.dot_general(spread, keys, NT, preferred_element_type=F32)
        score = score * (1.0 / math.sqrt(HEAD))
        scores.append(jnp.where(valid[lev * LEV_DEV + level] == 1, score, -1e30))
        value = lax.dot_general(value_t, block, NT, preferred_element_type=F32)
        values[level] = value.astype(BF16).astype(F32)
    top = functools.reduce(jnp.maximum, scores)
    expo = []
    for level in range(LEV_DEV):
        kept = valid[lev * LEV_DEV + level] == 1
        expo.append(jnp.where(kept, jnp.exp(scores[level] - top), 0.0))
    total = functools.reduce(jnp.add, expo)
    for level in range(LEV_DEV):
        weights[level] = expo[level] / total
    lse = top + jnp.log(total)

    place_here = jnp.where(lev % 2 == 0, lev // 2, (2 * LEV - 1 - lev) // 2)
    slots = [(place_here + LEV - 1 - RING.index(block)) % LEV for block in range(LEV)]
    for head in range(HEADS):
        for lane in range(0, CELLS, 128):
            lanes = pl.ds(lane, 128)
            terms = [
                values[level, pl.ds(head * HEAD, HEAD), lanes] for level in range(LEV_DEV)
            ]
            for latent in range(LATENTS):
                row = pl.ds(latent * HEADS + head, 1)
                summed = weights[0, row, lanes] * terms[0]
                for level in range(1, LEV_DEV):
                    summed = summed + weights[level, row, lanes] * terms[level]
                block, place = divmod(latent * HEADS + head, COMBOS)
                own[slots[block], pl.ds(place * HEAD, HEAD), lanes] = summed.astype(BF16)

    copies[4].wait()
    lane = lax.broadcasted_iota(jnp.int32, (SEC, CELLS), 1) + chunk * CELLS
    same = lane % SEC == lax.broadcasted_iota(jnp.int32, (SEC, CELLS), 0)
    same = jnp.logical_and(same, lane // SEC == lev)
    local = jnp.broadcast_to((partner[...] % SEC).astype(F32), (8, SEC)).astype(BF16)
    across = jnp.dot(local, jnp.where(same, 1.0, 0.0).astype(BF16), preferred_element_type=F32)
    for block in range(LEV):
        own[slots[block], pl.ds(FEATS, 16), :] = stat_rows(
            lse[block * COMBOS : (block + 1) * COMBOS], across[0:1]
        )
    first[...] = own[0]


def level_terms(chunk, *args):
    hbm = pl.BlockSpec(memory_space=pltpu.HBM)
    vmem = pl.BlockSpec(memory_space=pltpu.VMEM)
    return pl.pallas_call(
        functools.partial(level_kernel, chunk),
        out_shape=(
            jax.ShapeDtypeStruct((LEV, ROWS, CELLS), BF16),
            jax.ShapeDtypeStruct((ROWS, CELLS), BF16),
        ),
        in_specs=[hbm] * len(args),
        out_specs=(vmem, vmem),
        scratch_shapes=[
            pltpu.VMEM((LEV_DEV, E, CELLS), F32),
            pltpu.VMEM((LEV_DEV, LATENTS * HEADS, CELLS), F32),
            pltpu.SMEM((LEV * LEV_DEV,), jnp.int32),
            pltpu.VMEM((LATENTS, E), BF16),
            pltpu.VMEM((E, E), BF16),
            pltpu.VMEM((E, E), BF16),
            pltpu.VMEM((LEV_DEV, CELLS, E), BF16),
            pltpu.VMEM((1, SEC), jnp.int32),
            pltpu.SemaphoreType.DMA((5 + LEV_DEV,)),
        ],
        compiler_params=pltpu.CompilerParams(vmem_limit_bytes=LEVEL_LIMIT),
        name="level_terms",
    )(*args)


def merged(came, own, own_at=()):
    stats = came[pl.ds(FEATS, 16), :].astype(F32)
    mine = own[(*own_at, pl.ds(FEATS, 16), slice(None))].astype(F32)
    n = COMBOS
    there = stats[0:n] + stats[n : 2 * n] + stats[2 * n : 3 * n]
    here = mine[0:n] + mine[n : 2 * n] + mine[2 * n : 3 * n]
    best = jnp.maximum(there, here)
    grow = jnp.exp(there - best)
    total = grow + jnp.exp(here - best)
    share = grow / total
    partner = stats[3 * n : 3 * n + 1] + mine[3 * n : 3 * n + 1]
    blocks = []
    for place in range(COMBOS):
        rows = pl.ds(place * HEAD, HEAD)
        far = came[rows, :].astype(F32)
        near = own[(*own_at, rows, slice(None))].astype(F32)
        blocks.append(near + share[place : place + 1] * (far - near))
    return blocks, best + jnp.log(total), partner


def hop_kernel(step, came, own, out):
    blocks, lse, partner = merged(came, own, (step,))
    for place in range(COMBOS):
        out[pl.ds(place * HEAD, HEAD), :] = blocks[place].astype(BF16)
    out[pl.ds(FEATS, 16), :] = stat_rows(lse, partner)


def last_kernel(*refs):
    came, own, (out, across) = refs[:CHUNKS], refs[CHUNKS : 2 * CHUNKS], refs[2 * CHUNKS :]
    for chunk in range(CHUNKS):
        blocks, _, partner = merged(came[chunk], own[chunk], (LEV - 1,))
        lanes = pl.ds(chunk * CELLS, CELLS)
        for place in range(COMBOS):
            out[pl.ds(place * HEAD, HEAD), lanes] = blocks[place].astype(BF16)
        across[:, lanes] = jnp.broadcast_to(partner, (8, CELLS))


def vmem_call(kernel, out_shape, name, *args, scratch=()):
    vmem = pl.BlockSpec(memory_space=pltpu.VMEM)
    return pl.pallas_call(
        kernel,
        out_shape=out_shape,
        in_specs=[vmem] * len(args),
        out_specs=jax.tree.map(lambda _: vmem, out_shape),
        scratch_shapes=scratch,
        compiler_params=pltpu.CompilerParams(vmem_limit_bytes=VMEM_LIMIT),
        name=name,
    )(*args)


def pole_kernel(across, out):
    lane = lax.broadcasted_iota(jnp.int32, (1, NLON), 1)
    sector = (lane // SEC + LEV // 2) % LEV
    source = sector * SEC + across[0:1, :].astype(jnp.int32)
    place = lax.broadcasted_iota(jnp.int32, (NLON, NLON), 0)
    out[...] = jnp.where(place == source, 1.0, 0.0).astype(BF16)


def area_of(row):
    return math.cos(math.pi * (row + 0.5) / NLAT - math.pi / 2)


def coefficients(row):
    area, polar, inner = area_of(row), area_of(max(row - 1, 0)), area_of(row + 1)
    denom = 3.0 * area + polar + inner
    return area / denom, polar / denom, inner / denom


def diffuse_kernel(rows, halo, pole, out, raw, edge, one, two):
    south = lax.axis_index("half")
    raw[...] = rows[...].astype(F32)
    edge[...] = halo[...].astype(F32)

    def start(row):
        if row < GROUP:
            return raw[row + south * (GROUP - 1 - 2 * row)]
        k = row - GROUP
        return edge[k + south * (HOPS - 1 - 2 * k)]

    readers = (start, lambda row: one[row], lambda row: two[row])
    for step in range(HOPS):
        read = readers[step]
        here = read(0)
        high, mid, _ = pieces(here)
        both = jnp.concatenate([high, mid], axis=0).astype(BF16)
        turned = jnp.dot(both, pole[...], preferred_element_type=F32)
        before = turned[0:8] + turned[8:16]
        for row in range(GROUP + HOPS - 1 - step):
            after = read(row + 1)
            area, polar, inner = coefficients(row)
            beside = pltpu.roll(here, 1, 1) + pltpu.roll(here, NLON - 1, 1)
            state = area * (here + beside) + polar * before + inner * after
            if step == 0:
                one[row] = state
            elif step == 1:
                two[row] = state
            else:
                total = start(row) + one[row] + here + state
                raw[row + south * (GROUP - 1 - 2 * row)] = total * (1.0 / (HOPS + 1.0))
            before, here = here, after
    out[...] = raw[...].astype(BF16)


def diffuse(rows, halo, pole):
    scratch = [
        pltpu.VMEM((GROUP, 8, NLON), F32),
        pltpu.VMEM((HOPS, 8, NLON), F32),
        pltpu.VMEM((GROUP + HOPS, 8, NLON), F32),
        pltpu.VMEM((GROUP + HOPS, 8, NLON), F32),
    ]
    shape = jax.ShapeDtypeStruct(rows.shape, BF16)
    return vmem_call(diffuse_kernel, shape, "diffuse", rows, halo, pole, scratch=scratch)


def project_kernel(parts, weight, out):
    for latent in range(LATENTS):
        summed = jnp.dot(parts[2 * latent], weight[0:FEATS], preferred_element_type=F32)
        summed += jnp.dot(parts[2 * latent + 1], weight[FEATS:E], preferred_element_type=F32)
        out[0, :, pl.ds(latent * E, E)] = summed.astype(BF16)


def body(
    level_tokens, latent_queries, key_weight, value_weight, out_weight, level_valid, pole_partner
):
    south = lax.axis_index("half")
    tokens = jnp.transpose(level_tokens[0], (1, 0, 2))
    ring = [(RING[i], RING[(i + 1) % LEV]) for i in range(LEV)]
    message = jax.ShapeDtypeStruct((ROWS, CELLS), BF16)
    own, going = [], []
    for chunk in range(CHUNKS):
        terms, first = level_terms(
            chunk, level_valid, latent_queries, key_weight, value_weight, tokens,
            pole_partner[None],
        )
        own.append(terms)
        going.append(first)
    for step in range(1, LEV):
        came = [lax.ppermute(block, "lev", ring) for block in going]
        if step < LEV - 1:
            merge = functools.partial(hop_kernel, step)
            going = [
                vmem_call(merge, message, "hop", came[c], own[c]) for c in range(CHUNKS)
            ]
    pooled, across = vmem_call(
        last_kernel,
        (
            jax.ShapeDtypeStruct((FEATS, NLON), BF16),
            jax.ShapeDtypeStruct((8, NLON), F32),
        ),
        "last_hop",
        *came,
        *own,
    )

    rows = pooled.reshape(GROUP, FEATS // GROUP, NLON)
    rows = lax.all_to_all(rows, "row", split_axis=0, concat_axis=0, tiled=True)
    edge = jnp.where(south == 1, rows[:HOPS], rows[GROUP - HOPS :])
    halo = lax.ppermute(edge, "half", [(0, 1), (1, 0)])
    square = jax.ShapeDtypeStruct((NLON, NLON), BF16)
    pole = vmem_call(pole_kernel, square, "pole", across)
    mean = diffuse(rows, halo, pole)
    mean = lax.all_to_all(mean, "row", split_axis=0, concat_axis=0, tiled=True)
    sectors = mean.reshape(FEATS, NLON).T.reshape(LEV, SEC, FEATS)
    parts = lax.all_to_all(sectors, "lev", split_axis=0, concat_axis=0, tiled=True)
    shape = jax.ShapeDtypeStruct((1, SEC, LATENTS * E), BF16)
    return vmem_call(project_kernel, shape, "project", parts, out_weight)


def solution(mesh):
    halves = mesh.shape["lat"] // GROUP
    devices = mesh.devices.reshape(halves, GROUP, mesh.shape["lev"])
    mesh = Mesh(devices, ("half", "row", "lev"))
    lat = ("half", "row")
    in_specs = (P(lat, None, "lev", None), P(), P(), P(), P(), P(), P("lev"))
    out_specs = P(lat, "lev", None)
    return jax.shard_map(body, mesh=mesh, in_specs=in_specs, out_specs=out_specs, check_vma=False)
```

```python
import functools
import math

import jax
import jax.numpy as jnp
from jax import lax
from jax.experimental import pallas as pl
from jax.experimental.pallas import tpu as pltpu
from jax.sharding import Mesh
from jax.sharding import PartitionSpec as P

HEADS = 8
LATENTS = 4
HOPS = 3
E = 512
HEAD = E // HEADS
NLAT = 64
NLON = 512
LEV = 8
SEC = NLON // LEV
LEV_DEV = 5
GROUP = 32
FEATS = LATENTS * E // LEV
COMBOS = FEATS // HEAD
ROWS = FEATS + 16
RING = (0, 2, 4, 6, 7, 5, 3, 1)
F32 = jnp.float32
BF16 = jnp.bfloat16
NT = (((1,), (1,)), ((), ()))
VMEM_LIMIT = 8 * 1024 * 1024
LEVEL_LIMIT = 24 * 1024 * 1024


def pieces(x):
    high = x.astype(BF16).astype(F32)
    rest = x - high
    mid = rest.astype(BF16).astype(F32)
    return high, mid, rest - mid


def stat_rows(lse, partner):
    high, mid, low = pieces(lse)
    empty = jnp.zeros((16 - 3 * COMBOS - 1, lse.shape[1]), F32)
    return jnp.concatenate([high, mid, low, partner, empty], axis=0).astype(BF16)


def ring_place(lev):
    return jnp.where(lev % 2 == 0, lev // 2, (2 * LEV - 1 - lev) // 2)


def grouped_softmax(scores, valid, lev):
    kept = [valid[lev * LEV_DEV + level] == 1 for level in range(LEV_DEV)]
    masked = [jnp.where(keep, score, -1e30) for keep, score in zip(kept, scores)]
    top = functools.reduce(jnp.maximum, masked)
    expo = [jnp.where(keep, jnp.exp(score - top), 0.0) for keep, score in zip(kept, masked)]
    total = functools.reduce(jnp.add, expo)
    return [part / total for part in expo], top + jnp.log(total)


def partner_row(partner, lev):
    lane = lax.broadcasted_iota(jnp.int32, (SEC, NLON), 1)
    same = lane % SEC == lax.broadcasted_iota(jnp.int32, (SEC, NLON), 0)
    same = jnp.logical_and(same, lane // SEC == lev)
    local = jnp.broadcast_to((partner[...] % SEC).astype(F32), (8, SEC)).astype(BF16)
    spread = jnp.where(same, 1.0, 0.0).astype(BF16)
    return jnp.dot(local, spread, preferred_element_type=F32)[0:1]


def head_rows(query, latent_rows):
    width = query.shape[1]
    lane_head = lax.broadcasted_iota(jnp.int32, (HEADS, width), 1) // HEAD
    own_head = lane_head == lax.broadcasted_iota(jnp.int32, (HEADS, width), 0)
    rows = [jnp.where(own_head, row, 0.0) for row in latent_rows]
    return jnp.concatenate(rows, axis=0).astype(BF16)


def score_of(spread, block, key_weight):
    keys = jnp.dot(block, key_weight[...], preferred_element_type=F32).astype(BF16)
    score = lax.dot_general(spread, keys, NT, preferred_element_type=F32)
    return score * (1.0 / math.sqrt(HEAD))


def start_all(copies, fetches):
    for copy in copies[:4] + fetches + copies[4:]:
        copy.start()
    for copy in copies[:4]:
        copy.wait()


def first_kernel(
    valid_at, query_at, key_at, value_at, tokens_at, partner_at,
    first, valid, query, key_weight, value_weight, tokens, partner, sems,
):
    lev = lax.axis_index("lev")
    place = (ring_place(lev) + LEV - 1) % LEV
    block = jnp.where(place < LEV // 2, 2 * place, 2 * LEV - 1 - 2 * place)
    latent = block // 2
    columns = pl.ds(pl.multiple_of(block % 2 * FEATS, FEATS), FEATS)
    copies = [
        pltpu.make_async_copy(key_at.at[:, columns], key_weight, sems.at[0]),
        pltpu.make_async_copy(query_at.at[:, columns], query, sems.at[1]),
        pltpu.make_async_copy(valid_at, valid, sems.at[2]),
        pltpu.make_async_copy(value_at.at[:, columns], value_weight, sems.at[3]),
        pltpu.make_async_copy(partner_at, partner, sems.at[4]),
    ]
    fetches = [
        pltpu.make_async_copy(tokens_at.at[level], tokens.at[level], sems.at[5 + level])
        for level in range(LEV_DEV)
    ]
    start_all(copies, fetches)
    rows = query[...].astype(F32)
    row = functools.reduce(
        jnp.add, [jnp.where(latent == k, rows[k : k + 1], 0.0) for k in range(LATENTS)]
    )
    spread = head_rows(query, [row])
    value_t = value_weight[...].astype(F32).T.astype(BF16)
    scores, values = [], []
    for level in range(LEV_DEV):
        fetches[level].wait()
        here = tokens[level]
        scores.append(score_of(spread, here, key_weight))
        value = lax.dot_general(value_t, here, NT, preferred_element_type=F32)
        values.append(value.astype(BF16))
    weights, lse = grouped_softmax(scores, valid, lev)
    for place in range(COMBOS):
        rows = slice(place * HEAD, (place + 1) * HEAD)
        terms = [
            weights[level][place : place + 1] * values[level][rows].astype(F32)
            for level in range(LEV_DEV)
        ]
        first[pl.ds(place * HEAD, HEAD), :] = functools.reduce(jnp.add, terms).astype(BF16)
    copies[4].wait()
    first[pl.ds(FEATS, 16), :] = stat_rows(lse[0:COMBOS], partner_row(partner, lev))


def level_kernel(
    valid_at, query_at, key_at, value_at, tokens_at, partner_at,
    own, valid, query, key_weight, value_weight, tokens, partner, sems, values, weights,
):
    lev = lax.axis_index("lev")
    copies = [
        pltpu.make_async_copy(key_at, key_weight, sems.at[0]),
        pltpu.make_async_copy(query_at, query, sems.at[1]),
        pltpu.make_async_copy(valid_at, valid, sems.at[2]),
        pltpu.make_async_copy(value_at, value_weight, sems.at[3]),
        pltpu.make_async_copy(partner_at, partner, sems.at[4]),
    ]
    fetches = [
        pltpu.make_async_copy(tokens_at.at[level], tokens.at[level], sems.at[5 + level])
        for level in range(LEV_DEV)
    ]
    start_all(copies, fetches)
    rows = query[...].astype(F32)
    spread = head_rows(query, [rows[k : k + 1] for k in range(LATENTS)])
    value_t = value_weight[...].astype(F32).T.astype(BF16)
    scores = []
    for level in range(LEV_DEV):
        fetches[level].wait()
        here = tokens[level]
        scores.append(score_of(spread, here, key_weight))
        value = lax.dot_general(value_t, here, NT, preferred_element_type=F32)
        values[level] = value.astype(BF16).astype(F32)
    shares, lse = grouped_softmax(scores, valid, lev)
    for level in range(LEV_DEV):
        weights[level] = shares[level]

    slots = [(ring_place(lev) + LEV - 1 - RING.index(block)) % LEV for block in range(LEV)]
    for head in range(HEADS):
        for lane in range(0, NLON, 128):
            lanes = pl.ds(lane, 128)
            terms = [
                values[level, pl.ds(head * HEAD, HEAD), lanes] for level in range(LEV_DEV)
            ]
            for latent in range(LATENTS):
                row = pl.ds(latent * HEADS + head, 1)
                summed = weights[0, row, lanes] * terms[0]
                for level in range(1, LEV_DEV):
                    summed = summed + weights[level, row, lanes] * terms[level]
                block, place = divmod(latent * HEADS + head, COMBOS)
                own[slots[block], pl.ds(place * HEAD, HEAD), lanes] = summed.astype(BF16)
    copies[4].wait()
    across = partner_row(partner, lev)
    for block in range(LEV):
        own[slots[block], pl.ds(FEATS, 16), :] = stat_rows(
            lse[block * COMBOS : (block + 1) * COMBOS], across
        )


def level_call(kernel, shape, columns, scratch, name, args):
    hbm = pl.BlockSpec(memory_space=pltpu.HBM)
    return pl.pallas_call(
        kernel,
        out_shape=jax.ShapeDtypeStruct(shape, BF16),
        in_specs=[hbm] * len(args),
        out_specs=pl.BlockSpec(memory_space=pltpu.VMEM),
        scratch_shapes=[
            pltpu.SMEM((LEV * LEV_DEV,), jnp.int32),
            pltpu.VMEM((LATENTS, columns), BF16),
            pltpu.VMEM((E, columns), BF16),
            pltpu.VMEM((E, columns), BF16),
            pltpu.VMEM((LEV_DEV, NLON, E), BF16),
            pltpu.VMEM((1, SEC), jnp.int32),
            pltpu.SemaphoreType.DMA((5 + LEV_DEV,)),
            *scratch,
        ],
        compiler_params=pltpu.CompilerParams(vmem_limit_bytes=LEVEL_LIMIT),
        name=name,
    )(*[pltpu.with_memory_space_constraint(arg, pltpu.HBM) for arg in args])


def merged(came, own, own_at=()):
    stats = came[pl.ds(FEATS, 16), :].astype(F32)
    mine = own[(*own_at, pl.ds(FEATS, 16), slice(None))].astype(F32)
    n = COMBOS
    there = stats[0:n] + stats[n : 2 * n] + stats[2 * n : 3 * n]
    here = mine[0:n] + mine[n : 2 * n] + mine[2 * n : 3 * n]
    best = jnp.maximum(there, here)
    grow = jnp.exp(there - best)
    total = grow + jnp.exp(here - best)
    share = grow / total
    partner = stats[3 * n : 3 * n + 1] + mine[3 * n : 3 * n + 1]
    blocks = []
    for place in range(COMBOS):
        rows = pl.ds(place * HEAD, HEAD)
        far = came[rows, :].astype(F32)
        near = own[(*own_at, rows, slice(None))].astype(F32)
        blocks.append(near + share[place : place + 1] * (far - near))
    return blocks, best + jnp.log(total), partner


def hop_kernel(step, came, own, out):
    blocks, lse, partner = merged(came, own, (step,))
    for place in range(COMBOS):
        out[pl.ds(place * HEAD, HEAD), :] = blocks[place].astype(BF16)
    out[pl.ds(FEATS, 16), :] = stat_rows(lse, partner)


def last_kernel(came, own, out, across):
    blocks, _, partner = merged(came, own, (LEV - 1,))
    for place in range(COMBOS):
        out[pl.ds(place * HEAD, HEAD), :] = blocks[place].astype(BF16)
    across[...] = jnp.broadcast_to(partner, across.shape)


def vmem_call(kernel, out_shape, name, *args, scratch=()):
    vmem = pl.BlockSpec(memory_space=pltpu.VMEM)
    return pl.pallas_call(
        kernel,
        out_shape=out_shape,
        in_specs=[vmem] * len(args),
        out_specs=jax.tree.map(lambda _: vmem, out_shape),
        scratch_shapes=scratch,
        compiler_params=pltpu.CompilerParams(vmem_limit_bytes=VMEM_LIMIT),
        name=name,
    )(*args)


def pole_kernel(across, out):
    lane = lax.broadcasted_iota(jnp.int32, (1, NLON), 1)
    sector = (lane // SEC + LEV // 2) % LEV
    source = sector * SEC + across[0:1, :].astype(jnp.int32)
    place = lax.broadcasted_iota(jnp.int32, (NLON, NLON), 0)
    out[...] = jnp.where(place == source, 1.0, 0.0).astype(BF16)


def area_of(row):
    return math.cos(math.pi * (row + 0.5) / NLAT - math.pi / 2)


def coefficients(row):
    area, polar, inner = area_of(row), area_of(max(row - 1, 0)), area_of(row + 1)
    denom = 3.0 * area + polar + inner
    return area / denom, polar / denom, inner / denom


def diffuse_kernel(rows, halo, pole, out, raw, edge, one, two):
    south = lax.axis_index("half")
    raw[...] = rows[...].astype(F32)
    edge[...] = halo[...].astype(F32)

    def start(row):
        if row < GROUP:
            return raw[row + south * (GROUP - 1 - 2 * row)]
        k = row - GROUP
        return edge[k + south * (HOPS - 1 - 2 * k)]

    readers = (start, lambda row: one[row], lambda row: two[row])
    for step in range(HOPS):
        read = readers[step]
        here = read(0)
        high, mid, _ = pieces(here)
        both = jnp.concatenate([high, mid], axis=0).astype(BF16)
        turned = jnp.dot(both, pole[...], preferred_element_type=F32)
        before = turned[0:8] + turned[8:16]
        for row in range(GROUP + HOPS - 1 - step):
            after = read(row + 1)
            area, polar, inner = coefficients(row)
            beside = pltpu.roll(here, 1, 1) + pltpu.roll(here, NLON - 1, 1)
            state = area * (here + beside) + polar * before + inner * after
            if step == 0:
                one[row] = state
            elif step == 1:
                two[row] = state
            else:
                total = start(row) + one[row] + here + state
                raw[row + south * (GROUP - 1 - 2 * row)] = total * (1.0 / (HOPS + 1.0))
            before, here = here, after
    out[...] = raw[...].astype(BF16)


def diffuse(rows, halo, pole):
    scratch = [
        pltpu.VMEM((GROUP, 8, NLON), F32),
        pltpu.VMEM((HOPS, 8, NLON), F32),
        pltpu.VMEM((GROUP + HOPS, 8, NLON), F32),
        pltpu.VMEM((GROUP + HOPS, 8, NLON), F32),
    ]
    shape = jax.ShapeDtypeStruct(rows.shape, BF16)
    return vmem_call(diffuse_kernel, shape, "diffuse", rows, halo, pole, scratch=scratch)


def project_kernel(parts, weight, out):
    for latent in range(LATENTS):
        summed = jnp.dot(parts[2 * latent], weight[0:FEATS], preferred_element_type=F32)
        summed += jnp.dot(parts[2 * latent + 1], weight[FEATS:E], preferred_element_type=F32)
        out[0, :, pl.ds(latent * E, E)] = summed.astype(BF16)


def body(
    level_tokens, latent_queries, key_weight, value_weight, out_weight, level_valid, pole_partner
):
    south = lax.axis_index("half")
    tokens = jnp.transpose(level_tokens[0], (1, 0, 2))
    ring = [(RING[i], RING[(i + 1) % LEV]) for i in range(LEV)]
    args = (
        level_valid, latent_queries, key_weight, value_weight, tokens, pole_partner[None]
    )
    message = (ROWS, NLON)
    going = level_call(first_kernel, message, FEATS, (), "first_block", args)
    came = lax.ppermute(going, "lev", ring)
    scratch = (
        pltpu.VMEM((LEV_DEV, E, NLON), F32),
        pltpu.VMEM((LEV_DEV, LATENTS * HEADS, NLON), F32),
    )
    own = level_call(level_kernel, (LEV, *message), E, scratch, "all_blocks", args)
    for step in range(1, LEV - 1):
        merge = functools.partial(hop_kernel, step)
        going = vmem_call(merge, jax.ShapeDtypeStruct(message, BF16), "hop", came, own)
        came = lax.ppermute(going, "lev", ring)
    pooled, across = vmem_call(
        last_kernel,
        (
            jax.ShapeDtypeStruct((FEATS, NLON), BF16),
            jax.ShapeDtypeStruct((8, NLON), F32),
        ),
        "last_hop",
        came,
        own,
    )

    rows = pooled.reshape(GROUP, FEATS // GROUP, NLON)
    rows = lax.all_to_all(rows, "row", split_axis=0, concat_axis=0, tiled=True)
    edge = jnp.where(south == 1, rows[:HOPS], rows[GROUP - HOPS :])
    halo = lax.ppermute(edge, "half", [(0, 1), (1, 0)])
    square = jax.ShapeDtypeStruct((NLON, NLON), BF16)
    pole = vmem_call(pole_kernel, square, "pole", across)
    mean = diffuse(rows, halo, pole)
    mean = lax.all_to_all(mean, "row", split_axis=0, concat_axis=0, tiled=True)
    sectors = mean.reshape(FEATS, NLON).T.reshape(LEV, SEC, FEATS)
    parts = lax.all_to_all(sectors, "lev", split_axis=0, concat_axis=0, tiled=True)
    shape = jax.ShapeDtypeStruct((1, SEC, LATENTS * E), BF16)
    return vmem_call(project_kernel, shape, "project", parts, out_weight)


def solution(mesh):
    halves = mesh.shape["lat"] // GROUP
    devices = mesh.devices.reshape(halves, GROUP, mesh.shape["lev"])
    mesh = Mesh(devices, ("half", "row", "lev"))
    lat = ("half", "row")
    in_specs = (P(lat, None, "lev", None), P(), P(), P(), P(), P(), P("lev"))
    out_specs = P(lat, "lev", None)
    return jax.shard_map(body, mesh=mesh, in_specs=in_specs, out_specs=out_specs, check_vma=False)
```

```python
import functools
import math

import jax
import jax.numpy as jnp
from jax import lax
from jax.experimental import pallas as pl
from jax.experimental.pallas import tpu as pltpu
from jax.sharding import Mesh
from jax.sharding import PartitionSpec as P

HEADS = 8
LATENTS = 4
HOPS = 3
E = 512
HEAD = E // HEADS
NLAT = 64
NLON = 512
LEV = 8
SEC = NLON // LEV
LEV_DEV = 5
GROUP = 32
FEATS = LATENTS * E // LEV
COMBOS = FEATS // HEAD
ROWS = FEATS + 16
RING = (0, 2, 4, 6, 7, 5, 3, 1)
CHUNKS = 2
CELLS = NLON // CHUNKS
F32 = jnp.float32
BF16 = jnp.bfloat16
NT = (((1,), (1,)), ((), ()))
VMEM_LIMIT = 8 * 1024 * 1024
LEVEL_LIMIT = 24 * 1024 * 1024


def pieces(x):
    high = x.astype(BF16).astype(F32)
    rest = x - high
    mid = rest.astype(BF16).astype(F32)
    return high, mid, rest - mid


def stat_rows(lse, partner):
    high, mid, low = pieces(lse)
    empty = jnp.zeros((16 - 3 * COMBOS - 1, lse.shape[1]), F32)
    return jnp.concatenate([high, mid, low, partner, empty], axis=0).astype(BF16)


def block_of(lev):
    return (lev + lax.axis_index("half") * (LEV // 2)) % LEV


def ring_place(lev):
    return jnp.where(lev % 2 == 0, lev // 2, (2 * LEV - 1 - lev) // 2)


def grouped_softmax(scores, valid, lev):
    kept = [valid[lev * LEV_DEV + level] == 1 for level in range(LEV_DEV)]
    masked = [jnp.where(keep, score, -1e30) for keep, score in zip(kept, scores)]
    top = functools.reduce(jnp.maximum, masked)
    expo = [jnp.where(keep, jnp.exp(score - top), 0.0) for keep, score in zip(kept, masked)]
    total = functools.reduce(jnp.add, expo)
    return [part / total for part in expo], top + jnp.log(total)


def partner_row(partner, lev):
    lane = lax.broadcasted_iota(jnp.int32, (SEC, NLON), 1)
    same = lane % SEC == lax.broadcasted_iota(jnp.int32, (SEC, NLON), 0)
    same = jnp.logical_and(same, lane // SEC == lev)
    local = jnp.broadcast_to((partner[...] % SEC).astype(F32), (8, SEC)).astype(BF16)
    spread = jnp.where(same, 1.0, 0.0).astype(BF16)
    return jnp.dot(local, spread, preferred_element_type=F32)[0:1]


def head_rows(query, latent_rows):
    width = query.shape[1]
    lane_head = lax.broadcasted_iota(jnp.int32, (HEADS, width), 1) // HEAD
    own_head = lane_head == lax.broadcasted_iota(jnp.int32, (HEADS, width), 0)
    rows = [jnp.where(own_head, row, 0.0) for row in latent_rows]
    return jnp.concatenate(rows, axis=0).astype(BF16)


def score_of(spread, block, key_weight):
    keys = jnp.dot(block, key_weight[...], preferred_element_type=F32).astype(BF16)
    score = lax.dot_general(spread, keys, NT, preferred_element_type=F32)
    return score * (1.0 / math.sqrt(HEAD))


def start_all(copies, fetches):
    for copy in copies[:4] + fetches + copies[4:]:
        copy.start()
    for copy in copies[:4]:
        copy.wait()


def first_kernel(
    valid_at, query_at, key_at, value_at, tokens_at, partner_at,
    first, second, valid, query, key_weight, value_weight, tokens, partner, sems,
):
    lev = lax.axis_index("lev")
    place = (ring_place(lev) + LEV - 1) % LEV
    block = block_of(jnp.where(place < LEV // 2, 2 * place, 2 * LEV - 1 - 2 * place))
    latent = block // 2
    columns = pl.ds(pl.multiple_of(block % 2 * FEATS, FEATS), FEATS)
    copies = [
        pltpu.make_async_copy(key_at.at[:, columns], key_weight, sems.at[0]),
        pltpu.make_async_copy(query_at.at[:, columns], query, sems.at[1]),
        pltpu.make_async_copy(valid_at, valid, sems.at[2]),
        pltpu.make_async_copy(value_at.at[:, columns], value_weight, sems.at[3]),
        pltpu.make_async_copy(partner_at, partner, sems.at[4]),
    ]
    fetches = [
        pltpu.make_async_copy(tokens_at.at[level], tokens.at[level], sems.at[5 + level])
        for level in range(LEV_DEV)
    ]
    start_all(copies, fetches)
    rows = query[...].astype(F32)
    row = functools.reduce(
        jnp.add, [jnp.where(latent == k, rows[k : k + 1], 0.0) for k in range(LATENTS)]
    )
    spread = head_rows(query, [row])
    value_t = value_weight[...].astype(F32).T.astype(BF16)
    scores, values = [], []
    for level in range(LEV_DEV):
        fetches[level].wait()
        here = tokens[level]
        scores.append(score_of(spread, here, key_weight))
        value = lax.dot_general(value_t, here, NT, preferred_element_type=F32)
        values.append(value.astype(BF16))
    weights, lse = grouped_softmax(scores, valid, lev)
    for place in range(COMBOS):
        rows = slice(place * HEAD, (place + 1) * HEAD)
        terms = [
            weights[level][place : place + 1] * values[level][rows].astype(F32)
            for level in range(LEV_DEV)
        ]
        summed = functools.reduce(jnp.add, terms).astype(BF16)
        for chunk, out in enumerate((first, second)):
            lanes = slice(chunk * CELLS, (chunk + 1) * CELLS)
            out[pl.ds(place * HEAD, HEAD), :] = summed[:, lanes]
    copies[4].wait()
    stats = stat_rows(lse[0:COMBOS], partner_row(partner, lev))
    for chunk, out in enumerate((first, second)):
        out[pl.ds(FEATS, 16), :] = stats[:, chunk * CELLS : (chunk + 1) * CELLS]


def level_kernel(
    valid_at, query_at, key_at, value_at, tokens_at, partner_at,
    own, other, valid, query, key_weight, value_weight, tokens, partner, sems, values, weights,
):
    lev = lax.axis_index("lev")
    copies = [
        pltpu.make_async_copy(key_at, key_weight, sems.at[0]),
        pltpu.make_async_copy(query_at, query, sems.at[1]),
        pltpu.make_async_copy(valid_at, valid, sems.at[2]),
        pltpu.make_async_copy(value_at, value_weight, sems.at[3]),
        pltpu.make_async_copy(partner_at, partner, sems.at[4]),
    ]
    fetches = [
        pltpu.make_async_copy(tokens_at.at[level], tokens.at[level], sems.at[5 + level])
        for level in range(LEV_DEV)
    ]
    start_all(copies, fetches)
    rows = query[...].astype(F32)
    spread = head_rows(query, [rows[k : k + 1] for k in range(LATENTS)])
    value_t = value_weight[...].astype(F32).T.astype(BF16)
    scores = []
    for level in range(LEV_DEV):
        fetches[level].wait()
        here = tokens[level]
        scores.append(score_of(spread, here, key_weight))
        value = lax.dot_general(value_t, here, NT, preferred_element_type=F32)
        values[level] = value.astype(BF16).astype(F32)
    shares, lse = grouped_softmax(scores, valid, lev)
    for level in range(LEV_DEV):
        weights[level] = shares[level]

    here = ring_place(lev) + LEV - 1
    slots = [(here - ring_place(block_of(block))) % LEV for block in range(LEV)]
    for head in range(HEADS):
        for lane in range(0, NLON, 128):
            lanes = pl.ds(lane, 128)
            terms = [
                values[level, pl.ds(head * HEAD, HEAD), lanes] for level in range(LEV_DEV)
            ]
            for latent in range(LATENTS):
                row = pl.ds(latent * HEADS + head, 1)
                summed = weights[0, row, lanes] * terms[0]
                for level in range(1, LEV_DEV):
                    summed = summed + weights[level, row, lanes] * terms[level]
                block, place = divmod(latent * HEADS + head, COMBOS)
                out = (own, other)[lane // CELLS]
                lanes_out = pl.ds(lane % CELLS, 128)
                out[slots[block], pl.ds(place * HEAD, HEAD), lanes_out] = summed.astype(BF16)
    copies[4].wait()
    across = partner_row(partner, lev)
    for block in range(LEV):
        stats = stat_rows(lse[block * COMBOS : (block + 1) * COMBOS], across)
        for chunk, out in enumerate((own, other)):
            lanes = slice(chunk * CELLS, (chunk + 1) * CELLS)
            out[slots[block], pl.ds(FEATS, 16), :] = stats[:, lanes]


def level_call(kernel, shape, columns, scratch, name, args):
    hbm = pl.BlockSpec(memory_space=pltpu.HBM)
    return pl.pallas_call(
        kernel,
        out_shape=(jax.ShapeDtypeStruct(shape, BF16),) * CHUNKS,
        in_specs=[hbm] * len(args),
        out_specs=(pl.BlockSpec(memory_space=pltpu.VMEM),) * CHUNKS,
        scratch_shapes=[
            pltpu.SMEM((LEV * LEV_DEV,), jnp.int32),
            pltpu.VMEM((LATENTS, columns), BF16),
            pltpu.VMEM((E, columns), BF16),
            pltpu.VMEM((E, columns), BF16),
            pltpu.VMEM((LEV_DEV, NLON, E), BF16),
            pltpu.VMEM((1, SEC), jnp.int32),
            pltpu.SemaphoreType.DMA((5 + LEV_DEV,)),
            *scratch,
        ],
        compiler_params=pltpu.CompilerParams(vmem_limit_bytes=LEVEL_LIMIT),
        name=name,
    )(*[pltpu.with_memory_space_constraint(arg, pltpu.HBM) for arg in args])


def merged(came, own, own_at=()):
    stats = came[pl.ds(FEATS, 16), :].astype(F32)
    mine = own[(*own_at, pl.ds(FEATS, 16), slice(None))].astype(F32)
    n = COMBOS
    there = stats[0:n] + stats[n : 2 * n] + stats[2 * n : 3 * n]
    here = mine[0:n] + mine[n : 2 * n] + mine[2 * n : 3 * n]
    best = jnp.maximum(there, here)
    grow = jnp.exp(there - best)
    total = grow + jnp.exp(here - best)
    share = grow / total
    partner = stats[3 * n : 3 * n + 1] + mine[3 * n : 3 * n + 1]
    blocks = []
    for place in range(COMBOS):
        rows = pl.ds(place * HEAD, HEAD)
        far = came[rows, :].astype(F32)
        near = own[(*own_at, rows, slice(None))].astype(F32)
        blocks.append(near + share[place : place + 1] * (far - near))
    return blocks, best + jnp.log(total), partner


def hop_kernel(step, came, own, out):
    blocks, lse, partner = merged(came, own, (step,))
    for place in range(COMBOS):
        out[pl.ds(place * HEAD, HEAD), :] = blocks[place].astype(BF16)
    out[pl.ds(FEATS, 16), :] = stat_rows(lse, partner)


def last_kernel(*refs):
    came, own, (out, across) = refs[:CHUNKS], refs[CHUNKS : 2 * CHUNKS], refs[2 * CHUNKS :]
    for chunk in range(CHUNKS):
        blocks, _, partner = merged(came[chunk], own[chunk], (LEV - 1,))
        lanes = pl.ds(chunk * CELLS, CELLS)
        for place in range(COMBOS):
            out[pl.ds(place * HEAD, HEAD), lanes] = blocks[place].astype(BF16)
        across[:, lanes] = jnp.broadcast_to(partner, (8, CELLS))


def vmem_call(kernel, out_shape, name, *args, scratch=()):
    vmem = pl.BlockSpec(memory_space=pltpu.VMEM)
    return pl.pallas_call(
        kernel,
        out_shape=out_shape,
        in_specs=[vmem] * len(args),
        out_specs=jax.tree.map(lambda _: vmem, out_shape),
        scratch_shapes=scratch,
        compiler_params=pltpu.CompilerParams(vmem_limit_bytes=VMEM_LIMIT),
        name=name,
    )(*args)


def pole_kernel(across, out):
    lane = lax.broadcasted_iota(jnp.int32, (1, NLON), 1)
    sector = (lane // SEC + LEV // 2) % LEV
    source = sector * SEC + across[0:1, :].astype(jnp.int32)
    place = lax.broadcasted_iota(jnp.int32, (NLON, NLON), 0)
    out[...] = jnp.where(place == source, 1.0, 0.0).astype(BF16)


def area_of(row):
    return math.cos(math.pi * (row + 0.5) / NLAT - math.pi / 2)


def coefficients(row):
    area, polar, inner = area_of(row), area_of(max(row - 1, 0)), area_of(row + 1)
    denom = 3.0 * area + polar + inner
    return area / denom, polar / denom, inner / denom


def diffuse_kernel(rows, halo, pole, out, raw, edge, one, two):
    south = lax.axis_index("half")
    raw[...] = rows[...].astype(F32)
    edge[...] = halo[...].astype(F32)

    def start(row):
        if row < GROUP:
            return raw[row + south * (GROUP - 1 - 2 * row)]
        k = row - GROUP
        return edge[k + south * (HOPS - 1 - 2 * k)]

    readers = (start, lambda row: one[row], lambda row: two[row])
    for step in range(HOPS):
        read = readers[step]
        here = read(0)
        high, mid, _ = pieces(here)
        both = jnp.concatenate([high, mid], axis=0).astype(BF16)
        turned = jnp.dot(both, pole[...], preferred_element_type=F32)
        before = turned[0:8] + turned[8:16]
        for row in range(GROUP + HOPS - 1 - step):
            after = read(row + 1)
            area, polar, inner = coefficients(row)
            beside = pltpu.roll(here, 1, 1) + pltpu.roll(here, NLON - 1, 1)
            state = area * (here + beside) + polar * before + inner * after
            if step == 0:
                one[row] = state
            elif step == 1:
                two[row] = state
            else:
                total = start(row) + one[row] + here + state
                raw[row + south * (GROUP - 1 - 2 * row)] = total * (1.0 / (HOPS + 1.0))
            before, here = here, after
    out[...] = raw[...].astype(BF16)


def diffuse(rows, halo, pole):
    scratch = [
        pltpu.VMEM((GROUP, 8, NLON), F32),
        pltpu.VMEM((HOPS, 8, NLON), F32),
        pltpu.VMEM((GROUP + HOPS, 8, NLON), F32),
        pltpu.VMEM((GROUP + HOPS, 8, NLON), F32),
    ]
    shape = jax.ShapeDtypeStruct(rows.shape, BF16)
    return vmem_call(diffuse_kernel, shape, "diffuse", rows, halo, pole, scratch=scratch)


def project_kernel(parts, weight, out):
    for latent in range(LATENTS):
        low, high = parts[block_of(2 * latent)], parts[block_of(2 * latent + 1)]
        summed = jnp.dot(low, weight[0:FEATS], preferred_element_type=F32)
        summed += jnp.dot(high, weight[FEATS:E], preferred_element_type=F32)
        out[0, :, pl.ds(latent * E, E)] = summed.astype(BF16)


def body(
    level_tokens, latent_queries, key_weight, value_weight, out_weight, level_valid, pole_partner
):
    south = lax.axis_index("half")
    tokens = jnp.transpose(level_tokens[0], (1, 0, 2))
    ring = [(RING[i], RING[(i + 1) % LEV]) for i in range(LEV)]
    args = (
        level_valid, latent_queries, key_weight, value_weight, tokens, pole_partner[None]
    )
    message = (ROWS, CELLS)
    going = level_call(first_kernel, message, FEATS, (), "first_block", args)
    came = [lax.ppermute(block, "lev", ring) for block in going]
    scratch = (
        pltpu.VMEM((LEV_DEV, E, NLON), F32),
        pltpu.VMEM((LEV_DEV, LATENTS * HEADS, NLON), F32),
    )
    own = level_call(level_kernel, (LEV, *message), E, scratch, "all_blocks", args)
    for step in range(1, LEV - 1):
        merge = functools.partial(hop_kernel, step)
        shape = jax.ShapeDtypeStruct(message, BF16)
        going = [vmem_call(merge, shape, "hop", came[c], own[c]) for c in range(CHUNKS)]
        came = [lax.ppermute(block, "lev", ring) for block in going]
    pooled, across = vmem_call(
        last_kernel,
        (
            jax.ShapeDtypeStruct((FEATS, NLON), BF16),
            jax.ShapeDtypeStruct((8, NLON), F32),
        ),
        "last_hop",
        *came,
        *own,
    )

    rows = pooled.reshape(GROUP, FEATS // GROUP, NLON)
    rows = lax.all_to_all(rows, "row", split_axis=0, concat_axis=0, tiled=True)
    edge = jnp.where(south == 1, rows[:HOPS], rows[GROUP - HOPS :])
    turned = [(lev, LEV + (lev + LEV // 2) % LEV) for lev in range(LEV)]
    turned += [(there, here) for here, there in turned]
    halo = lax.ppermute(edge, ("half", "lev"), turned)
    square = jax.ShapeDtypeStruct((NLON, NLON), BF16)
    pole = vmem_call(pole_kernel, square, "pole", across)
    mean = diffuse(rows, halo, pole)
    mean = lax.all_to_all(mean, "row", split_axis=0, concat_axis=0, tiled=True)
    sectors = mean.reshape(FEATS, NLON).T.reshape(LEV, SEC, FEATS)
    parts = lax.all_to_all(sectors, "lev", split_axis=0, concat_axis=0, tiled=True)
    shape = jax.ShapeDtypeStruct((1, SEC, LATENTS * E), BF16)
    return vmem_call(project_kernel, shape, "project", parts, out_weight)


def solution(mesh):
    halves = mesh.shape["lat"] // GROUP
    devices = mesh.devices.reshape(halves, GROUP, mesh.shape["lev"])
    mesh = Mesh(devices, ("half", "row", "lev"))
    lat = ("half", "row")
    in_specs = (P(lat, None, "lev", None), P(), P(), P(), P(), P(), P("lev"))
    out_specs = P(lat, "lev", None)
    return jax.shard_map(body, mesh=mesh, in_specs=in_specs, out_specs=out_specs, check_vma=False)
```

```python
import functools
import math

import jax
import jax.numpy as jnp
from jax import lax
from jax.experimental import pallas as pl
from jax.experimental.pallas import tpu as pltpu
from jax.sharding import Mesh
from jax.sharding import PartitionSpec as P

HEADS = 8
LATENTS = 4
HOPS = 3
E = 512
HEAD = E // HEADS
NLAT = 64
NLON = 512
LEV = 8
SEC = NLON // LEV
LEV_DEV = 5
GROUP = 32
FEATS = LATENTS * E // LEV
COMBOS = FEATS // HEAD
ROWS = FEATS + 16
RING = (0, 2, 4, 6, 7, 5, 3, 1)
CHUNKS = 2
CELLS = NLON // CHUNKS
F32 = jnp.float32
BF16 = jnp.bfloat16
NT = (((1,), (1,)), ((), ()))
VMEM_LIMIT = 8 * 1024 * 1024
LEVEL_LIMIT = 24 * 1024 * 1024


def pieces(x):
    high = x.astype(BF16).astype(F32)
    rest = x - high
    mid = rest.astype(BF16).astype(F32)
    return high, mid, rest - mid


def stat_rows(lse, partner):
    high, mid, low = pieces(lse)
    empty = jnp.zeros((16 - 3 * COMBOS - 1, lse.shape[1]), F32)
    return jnp.concatenate([high, mid, low, partner, empty], axis=0).astype(BF16)


def block_of(lev):
    return (lev + lax.axis_index("half") * (LEV // 2)) % LEV


def ring_place(lev):
    return jnp.where(lev % 2 == 0, lev // 2, (2 * LEV - 1 - lev) // 2)


def grouped_softmax(scores, valid, lev):
    kept = [valid[lev * LEV_DEV + level] == 1 for level in range(LEV_DEV)]
    masked = [jnp.where(keep, score, -1e30) for keep, score in zip(kept, scores)]
    top = functools.reduce(jnp.maximum, masked)
    expo = [jnp.where(keep, jnp.exp(score - top), 0.0) for keep, score in zip(kept, masked)]
    total = functools.reduce(jnp.add, expo)
    return [part / total for part in expo], top + jnp.log(total)


def partner_row(partner, lev):
    lane = lax.broadcasted_iota(jnp.int32, (SEC, NLON), 1)
    same = lane % SEC == lax.broadcasted_iota(jnp.int32, (SEC, NLON), 0)
    same = jnp.logical_and(same, lane // SEC == lev)
    local = jnp.broadcast_to((partner[...] % SEC).astype(F32), (8, SEC)).astype(BF16)
    spread = jnp.where(same, 1.0, 0.0).astype(BF16)
    return jnp.dot(local, spread, preferred_element_type=F32)[0:1]


def head_rows(query, latent_rows):
    width = query.shape[1]
    lane_head = lax.broadcasted_iota(jnp.int32, (HEADS, width), 1) // HEAD
    own_head = lane_head == lax.broadcasted_iota(jnp.int32, (HEADS, width), 0)
    rows = [jnp.where(own_head, row, 0.0) for row in latent_rows]
    return jnp.concatenate(rows, axis=0).astype(BF16)


def score_of(spread, block, key_weight):
    keys = jnp.dot(block, key_weight[...], preferred_element_type=F32).astype(BF16)
    score = lax.dot_general(spread, keys, NT, preferred_element_type=F32)
    return score * (1.0 / math.sqrt(HEAD))


def first_kernel(
    valid_at, query_at, key_at, value_at, tokens_at, partner_at,
    first, second, values, weights, stats,
    valid, query, key_weight, value_weight, tokens, partner, sems,
):
    lev = lax.axis_index("lev")
    copies = [
        pltpu.make_async_copy(key_at, key_weight, sems.at[0]),
        pltpu.make_async_copy(value_at, value_weight, sems.at[1]),
        pltpu.make_async_copy(query_at, query, sems.at[2]),
        pltpu.make_async_copy(valid_at, valid, sems.at[3]),
        pltpu.make_async_copy(partner_at, partner, sems.at[4]),
    ]
    fetches = [
        pltpu.make_async_copy(tokens_at.at[level], tokens.at[level], sems.at[5 + level])
        for level in range(LEV_DEV)
    ]
    for copy in copies + fetches:
        copy.start()
    for copy in copies:
        copy.wait()
    rows = query[...].astype(F32)
    spread = head_rows(query, [rows[k : k + 1] for k in range(LATENTS)])
    value_t = value_weight[...].astype(F32).T.astype(BF16)
    scores = []
    for level in range(LEV_DEV):
        fetches[level].wait()
        here = tokens[level]
        scores.append(score_of(spread, here, key_weight))
        value = lax.dot_general(value_t, here, NT, preferred_element_type=F32)
        values[level] = value.astype(BF16).astype(F32)
    shares, lse = grouped_softmax(scores, valid, lev)
    for level in range(LEV_DEV):
        weights[level] = shares[level]
    across = partner_row(partner, lev)
    for block in range(LEV):
        stats[block] = stat_rows(lse[block * COMBOS : (block + 1) * COMBOS], across)

    place = (ring_place(lev) + LEV - 1) % LEV
    block = block_of(jnp.where(place < LEV // 2, 2 * place, 2 * LEV - 1 - 2 * place))
    for chunk, out in enumerate((first, second)):
        lanes = pl.ds(chunk * CELLS, CELLS)
        for place in range(COMBOS):
            head = pl.multiple_of((block % 2 * COMBOS + place) * HEAD, HEAD)
            row = pl.ds(block * COMBOS + place, 1)
            terms = [
                weights[level, row, lanes] * values[level, pl.ds(head, HEAD), lanes]
                for level in range(LEV_DEV)
            ]
            summed = functools.reduce(jnp.add, terms)
            out[pl.ds(place * HEAD, HEAD), :] = summed.astype(BF16)
        out[pl.ds(FEATS, 16), :] = stats[block, :, lanes]


def first_block(*args):
    hbm = pl.BlockSpec(memory_space=pltpu.HBM)
    vmem = pl.BlockSpec(memory_space=pltpu.VMEM)
    return pl.pallas_call(
        first_kernel,
        out_shape=(
            jax.ShapeDtypeStruct((ROWS, CELLS), BF16),
            jax.ShapeDtypeStruct((ROWS, CELLS), BF16),
            jax.ShapeDtypeStruct((LEV_DEV, E, NLON), F32),
            jax.ShapeDtypeStruct((LEV_DEV, LATENTS * HEADS, NLON), F32),
            jax.ShapeDtypeStruct((LEV, 16, NLON), BF16),
        ),
        in_specs=[hbm] * len(args),
        out_specs=(vmem,) * 5,
        scratch_shapes=[
            pltpu.SMEM((LEV * LEV_DEV,), jnp.int32),
            pltpu.VMEM((LATENTS, E), BF16),
            pltpu.VMEM((E, E), BF16),
            pltpu.VMEM((E, E), BF16),
            pltpu.VMEM((LEV_DEV, NLON, E), BF16),
            pltpu.VMEM((1, SEC), jnp.int32),
            pltpu.SemaphoreType.DMA((5 + LEV_DEV,)),
        ],
        compiler_params=pltpu.CompilerParams(vmem_limit_bytes=LEVEL_LIMIT),
        name="first_block",
    )(*[pltpu.with_memory_space_constraint(arg, pltpu.HBM) for arg in args])


def blocks_kernel(values, weights, stats, own, other):
    lev = lax.axis_index("lev")
    here = ring_place(lev) + LEV - 1
    slots = [(here - ring_place(block_of(block))) % LEV for block in range(LEV)]
    for head in range(HEADS):
        for lane in range(0, NLON, 128):
            lanes = pl.ds(lane, 128)
            terms = [
                values[level, pl.ds(head * HEAD, HEAD), lanes] for level in range(LEV_DEV)
            ]
            for latent in range(LATENTS):
                row = pl.ds(latent * HEADS + head, 1)
                summed = weights[0, row, lanes] * terms[0]
                for level in range(1, LEV_DEV):
                    summed = summed + weights[level, row, lanes] * terms[level]
                block, place = divmod(latent * HEADS + head, COMBOS)
                out = (own, other)[lane // CELLS]
                lanes_out = pl.ds(lane % CELLS, 128)
                out[slots[block], pl.ds(place * HEAD, HEAD), lanes_out] = summed.astype(BF16)
    for block in range(LEV):
        for chunk, out in enumerate((own, other)):
            lanes = pl.ds(chunk * CELLS, CELLS)
            out[slots[block], pl.ds(FEATS, 16), :] = stats[block, :, lanes]


def merged(came, own, own_at=()):
    stats = came[pl.ds(FEATS, 16), :].astype(F32)
    mine = own[(*own_at, pl.ds(FEATS, 16), slice(None))].astype(F32)
    n = COMBOS
    there = stats[0:n] + stats[n : 2 * n] + stats[2 * n : 3 * n]
    here = mine[0:n] + mine[n : 2 * n] + mine[2 * n : 3 * n]
    best = jnp.maximum(there, here)
    grow = jnp.exp(there - best)
    total = grow + jnp.exp(here - best)
    share = grow / total
    partner = stats[3 * n : 3 * n + 1] + mine[3 * n : 3 * n + 1]
    blocks = []
    for place in range(COMBOS):
        rows = pl.ds(place * HEAD, HEAD)
        far = came[rows, :].astype(F32)
        near = own[(*own_at, rows, slice(None))].astype(F32)
        blocks.append(near + share[place : place + 1] * (far - near))
    return blocks, best + jnp.log(total), partner


def hop_kernel(step, came, own, out):
    blocks, lse, partner = merged(came, own, (step,))
    for place in range(COMBOS):
        out[pl.ds(place * HEAD, HEAD), :] = blocks[place].astype(BF16)
    out[pl.ds(FEATS, 16), :] = stat_rows(lse, partner)


def last_kernel(*refs):
    came, own, (out, across) = refs[:CHUNKS], refs[CHUNKS : 2 * CHUNKS], refs[2 * CHUNKS :]
    for chunk in range(CHUNKS):
        blocks, _, partner = merged(came[chunk], own[chunk], (LEV - 1,))
        lanes = pl.ds(chunk * CELLS, CELLS)
        for place in range(COMBOS):
            out[pl.ds(place * HEAD, HEAD), lanes] = blocks[place].astype(BF16)
        across[:, lanes] = jnp.broadcast_to(partner, (8, CELLS))


def vmem_call(kernel, out_shape, name, *args, scratch=()):
    vmem = pl.BlockSpec(memory_space=pltpu.VMEM)
    return pl.pallas_call(
        kernel,
        out_shape=out_shape,
        in_specs=[vmem] * len(args),
        out_specs=jax.tree.map(lambda _: vmem, out_shape),
        scratch_shapes=scratch,
        compiler_params=pltpu.CompilerParams(vmem_limit_bytes=VMEM_LIMIT),
        name=name,
    )(*args)


def pole_matrix(across):
    lane = lax.broadcasted_iota(jnp.int32, (1, NLON), 1)
    sector = (lane // SEC + LEV // 2) % LEV
    source = sector * SEC + across[0:1, :].astype(jnp.int32)
    place = lax.broadcasted_iota(jnp.int32, (NLON, NLON), 0)
    return jnp.where(place == source, 1.0, 0.0).astype(BF16)


def area_of(row):
    return math.cos(math.pi * (row + 0.5) / NLAT - math.pi / 2)


def coefficients(row):
    area, polar, inner = area_of(row), area_of(max(row - 1, 0)), area_of(row + 1)
    denom = 3.0 * area + polar + inner
    return area / denom, polar / denom, inner / denom


def diffuse_kernel(rows, halo, across, out, raw, edge, one, two, pole):
    south = lax.axis_index("half")
    raw[...] = rows[...].astype(F32)
    edge[...] = halo[...].astype(F32)
    pole[...] = pole_matrix(across)

    def start(row):
        if row < GROUP:
            return raw[row + south * (GROUP - 1 - 2 * row)]
        k = row - GROUP
        return edge[k + south * (HOPS - 1 - 2 * k)]

    readers = (start, lambda row: one[row], lambda row: two[row])
    for step in range(HOPS):
        read = readers[step]
        here = read(0)
        high, mid, _ = pieces(here)
        both = jnp.concatenate([high, mid], axis=0).astype(BF16)
        turned = jnp.dot(both, pole[...], preferred_element_type=F32)
        before = turned[0:8] + turned[8:16]
        for row in range(GROUP + HOPS - 1 - step):
            after = read(row + 1)
            area, polar, inner = coefficients(row)
            beside = pltpu.roll(here, 1, 1) + pltpu.roll(here, NLON - 1, 1)
            state = area * (here + beside) + polar * before + inner * after
            if step == 0:
                one[row] = state
            elif step == 1:
                two[row] = state
            else:
                total = start(row) + one[row] + here + state
                raw[row + south * (GROUP - 1 - 2 * row)] = total * (1.0 / (HOPS + 1.0))
            before, here = here, after
    out[...] = raw[...].astype(BF16)


def diffuse(rows, halo, across):
    scratch = [
        pltpu.VMEM((GROUP, 8, NLON), F32),
        pltpu.VMEM((HOPS, 8, NLON), F32),
        pltpu.VMEM((GROUP + HOPS, 8, NLON), F32),
        pltpu.VMEM((GROUP + HOPS, 8, NLON), F32),
        pltpu.VMEM((NLON, NLON), BF16),
    ]
    shape = jax.ShapeDtypeStruct(rows.shape, BF16)
    return vmem_call(diffuse_kernel, shape, "diffuse", rows, halo, across, scratch=scratch)


def project_kernel(parts, weight, out):
    for latent in range(LATENTS):
        low, high = parts[block_of(2 * latent)], parts[block_of(2 * latent + 1)]
        summed = jnp.dot(low, weight[0:FEATS], preferred_element_type=F32)
        summed += jnp.dot(high, weight[FEATS:E], preferred_element_type=F32)
        out[0, :, pl.ds(latent * E, E)] = summed.astype(BF16)


def body(
    level_tokens, latent_queries, key_weight, value_weight, out_weight, level_valid, pole_partner
):
    south = lax.axis_index("half")
    tokens = jnp.transpose(level_tokens[0], (1, 0, 2))
    ring = [(RING[i], RING[(i + 1) % LEV]) for i in range(LEV)]
    args = (
        level_valid, latent_queries, key_weight, value_weight, tokens, pole_partner[None]
    )
    message = (ROWS, CELLS)
    *going, values, weights, stats = first_block(*args)
    came = [lax.ppermute(block, "lev", ring) for block in going]
    shapes = (jax.ShapeDtypeStruct((LEV, *message), BF16),) * CHUNKS
    own = vmem_call(blocks_kernel, shapes, "all_blocks", values, weights, stats)
    for step in range(1, LEV - 1):
        merge = functools.partial(hop_kernel, step)
        shape = jax.ShapeDtypeStruct(message, BF16)
        going = [vmem_call(merge, shape, "hop", came[c], own[c]) for c in range(CHUNKS)]
        came = [lax.ppermute(block, "lev", ring) for block in going]
    pooled, across = vmem_call(
        last_kernel,
        (
            jax.ShapeDtypeStruct((FEATS, NLON), BF16),
            jax.ShapeDtypeStruct((8, NLON), F32),
        ),
        "last_hop",
        *came,
        *own,
    )

    rows = pooled.reshape(GROUP, FEATS // GROUP, NLON)
    rows = lax.all_to_all(rows, "row", split_axis=0, concat_axis=0, tiled=True)
    edge = jnp.where(south == 1, rows[:HOPS], rows[GROUP - HOPS :])
    turned = [(lev, LEV + (lev + LEV // 2) % LEV) for lev in range(LEV)]
    turned += [(there, here) for here, there in turned]
    halo = lax.ppermute(edge, ("half", "lev"), turned)
    mean = diffuse(rows, halo, across)
    mean = lax.all_to_all(mean, "row", split_axis=0, concat_axis=0, tiled=True)
    sectors = mean.reshape(FEATS, NLON).T.reshape(LEV, SEC, FEATS)
    parts = lax.all_to_all(sectors, "lev", split_axis=0, concat_axis=0, tiled=True)
    shape = jax.ShapeDtypeStruct((1, SEC, LATENTS * E), BF16)
    return vmem_call(project_kernel, shape, "project", parts, out_weight)


def solution(mesh):
    halves = mesh.shape["lat"] // GROUP
    devices = mesh.devices.reshape(halves, GROUP, mesh.shape["lev"])
    mesh = Mesh(devices, ("half", "row", "lev"))
    lat = ("half", "row")
    in_specs = (P(lat, None, "lev", None), P(), P(), P(), P(), P(), P("lev"))
    out_specs = P(lat, "lev", None)
    return jax.shard_map(body, mesh=mesh, in_specs=in_specs, out_specs=out_specs, check_vma=False)
```

```python
import functools
import math

import jax
import jax.numpy as jnp
from jax import lax
from jax.experimental import pallas as pl
from jax.experimental.pallas import tpu as pltpu
from jax.sharding import Mesh
from jax.sharding import PartitionSpec as P

HEADS = 8
LATENTS = 4
HOPS = 3
E = 512
HEAD = E // HEADS
NLAT = 64
NLON = 512
LEV = 8
SEC = NLON // LEV
LEV_DEV = 5
GROUP = 32
FEATS = LATENTS * E // LEV
COMBOS = FEATS // HEAD
ROWS = FEATS + 16
RING = (0, 2, 4, 6, 7, 5, 3, 1)
CHUNKS = 2
CELLS = NLON // CHUNKS
F32 = jnp.float32
BF16 = jnp.bfloat16
NT = (((1,), (1,)), ((), ()))
VMEM_LIMIT = 8 * 1024 * 1024
LEVEL_LIMIT = 24 * 1024 * 1024


def pieces(x):
    high = x.astype(BF16).astype(F32)
    rest = x - high
    mid = rest.astype(BF16).astype(F32)
    return high, mid, rest - mid


def stat_rows(lse, partner):
    high, mid, low = pieces(lse)
    empty = jnp.zeros((16 - 3 * COMBOS - 1, lse.shape[1]), F32)
    return jnp.concatenate([high, mid, low, partner, empty], axis=0).astype(BF16)


def block_of(lev):
    return (lev + lax.axis_index("half") * (LEV // 2)) % LEV


def ring_place(lev):
    return jnp.where(lev % 2 == 0, lev // 2, (2 * LEV - 1 - lev) // 2)


def grouped_softmax(scores, valid, lev):
    kept = [valid[lev * LEV_DEV + level] == 1 for level in range(LEV_DEV)]
    masked = [jnp.where(keep, score, -1e30) for keep, score in zip(kept, scores)]
    top = functools.reduce(jnp.maximum, masked)
    expo = [jnp.where(keep, jnp.exp(score - top), 0.0) for keep, score in zip(kept, masked)]
    total = functools.reduce(jnp.add, expo)
    return [part / total for part in expo], top + jnp.log(total)


def partner_row(partner, lev):
    lane = lax.broadcasted_iota(jnp.int32, (SEC, NLON), 1)
    same = lane % SEC == lax.broadcasted_iota(jnp.int32, (SEC, NLON), 0)
    same = jnp.logical_and(same, lane // SEC == lev)
    local = jnp.broadcast_to((partner[...] % SEC).astype(F32), (8, SEC)).astype(BF16)
    spread = jnp.where(same, 1.0, 0.0).astype(BF16)
    return jnp.dot(local, spread, preferred_element_type=F32)[0:1]


def head_rows(query, latent_rows):
    width = query.shape[1]
    lane_head = lax.broadcasted_iota(jnp.int32, (HEADS, width), 1) // HEAD
    own_head = lane_head == lax.broadcasted_iota(jnp.int32, (HEADS, width), 0)
    rows = [jnp.where(own_head, row, 0.0) for row in latent_rows]
    return jnp.concatenate(rows, axis=0).astype(BF16)


def score_of(spread, block, key_weight):
    keys = jnp.dot(block, key_weight[...], preferred_element_type=F32).astype(BF16)
    score = lax.dot_general(spread, keys, NT, preferred_element_type=F32)
    return score * (1.0 / math.sqrt(HEAD))


def first_kernel(
    valid_at, query_at, key_at, value_at, tokens_at, partner_at,
    first, second, values, weights, stats,
    valid, query, key_weight, value_weight, tokens, partner, sems,
):
    lev = lax.axis_index("lev")
    copies = [
        pltpu.make_async_copy(key_at, key_weight, sems.at[0]),
        pltpu.make_async_copy(value_at, value_weight, sems.at[1]),
        pltpu.make_async_copy(query_at, query, sems.at[2]),
        pltpu.make_async_copy(valid_at, valid, sems.at[3]),
        pltpu.make_async_copy(partner_at, partner, sems.at[4]),
    ]
    fetches = [
        pltpu.make_async_copy(tokens_at.at[level], tokens.at[level], sems.at[5 + level])
        for level in range(LEV_DEV)
    ]
    for copy in copies + fetches:
        copy.start()
    for copy in copies:
        copy.wait()
    rows = query[...].astype(F32)
    spread = head_rows(query, [rows[k : k + 1] for k in range(LATENTS)])
    value_t = value_weight[...].astype(F32).T.astype(BF16)
    scores = []
    for level in range(LEV_DEV):
        fetches[level].wait()
        here = tokens[level]
        scores.append(score_of(spread, here, key_weight))
        value = lax.dot_general(value_t, here, NT, preferred_element_type=F32)
        values[level] = value.astype(BF16).astype(F32)
    shares, lse = grouped_softmax(scores, valid, lev)
    for level in range(LEV_DEV):
        weights[level] = shares[level]
    across = partner_row(partner, lev)
    for block in range(LEV):
        stats[block] = stat_rows(lse[block * COMBOS : (block + 1) * COMBOS], across)

    place = (ring_place(lev) + LEV - 1) % LEV
    block = block_of(jnp.where(place < LEV // 2, 2 * place, 2 * LEV - 1 - 2 * place))
    for chunk, out in enumerate((first, second)):
        lanes = pl.ds(chunk * CELLS, CELLS)
        for place in range(COMBOS):
            head = pl.multiple_of((block % 2 * COMBOS + place) * HEAD, HEAD)
            row = pl.ds(block * COMBOS + place, 1)
            terms = [
                weights[level, row, lanes] * values[level, pl.ds(head, HEAD), lanes]
                for level in range(LEV_DEV)
            ]
            summed = functools.reduce(jnp.add, terms)
            out[pl.ds(place * HEAD, HEAD), :] = summed.astype(BF16)
        out[pl.ds(FEATS, 16), :] = stats[block, :, lanes]


def first_block(*args):
    hbm = pl.BlockSpec(memory_space=pltpu.HBM)
    vmem = pl.BlockSpec(memory_space=pltpu.VMEM)
    return pl.pallas_call(
        first_kernel,
        out_shape=(
            jax.ShapeDtypeStruct((ROWS, CELLS), BF16),
            jax.ShapeDtypeStruct((ROWS, CELLS), BF16),
            jax.ShapeDtypeStruct((LEV_DEV, E, NLON), F32),
            jax.ShapeDtypeStruct((LEV_DEV, LATENTS * HEADS, NLON), F32),
            jax.ShapeDtypeStruct((LEV, 16, NLON), BF16),
        ),
        in_specs=[hbm] * len(args),
        out_specs=(vmem,) * 5,
        scratch_shapes=[
            pltpu.SMEM((LEV * LEV_DEV,), jnp.int32),
            pltpu.VMEM((LATENTS, E), BF16),
            pltpu.VMEM((E, E), BF16),
            pltpu.VMEM((E, E), BF16),
            pltpu.VMEM((LEV_DEV, NLON, E), BF16),
            pltpu.VMEM((1, SEC), jnp.int32),
            pltpu.SemaphoreType.DMA((5 + LEV_DEV,)),
        ],
        compiler_params=pltpu.CompilerParams(vmem_limit_bytes=LEVEL_LIMIT),
        name="first_block",
    )(*[pltpu.with_memory_space_constraint(arg, pltpu.HBM) for arg in args])


def blocks_kernel(values, weights, stats, own, other):
    lev = lax.axis_index("lev")
    here = ring_place(lev) + LEV - 1
    slots = [(here - ring_place(block_of(block))) % LEV for block in range(LEV)]
    for head in range(HEADS):
        for lane in range(0, NLON, 128):
            lanes = pl.ds(lane, 128)
            terms = [
                values[level, pl.ds(head * HEAD, HEAD), lanes] for level in range(LEV_DEV)
            ]
            for latent in range(LATENTS):
                row = pl.ds(latent * HEADS + head, 1)
                summed = weights[0, row, lanes] * terms[0]
                for level in range(1, LEV_DEV):
                    summed = summed + weights[level, row, lanes] * terms[level]
                block, place = divmod(latent * HEADS + head, COMBOS)
                out = (own, other)[lane // CELLS]
                lanes_out = pl.ds(lane % CELLS, 128)
                out[slots[block], pl.ds(place * HEAD, HEAD), lanes_out] = summed.astype(BF16)
    for block in range(LEV):
        for chunk, out in enumerate((own, other)):
            lanes = pl.ds(chunk * CELLS, CELLS)
            out[slots[block], pl.ds(FEATS, 16), :] = stats[block, :, lanes]


def merged(came, own, own_at=()):
    stats = came[pl.ds(FEATS, 16), :].astype(F32)
    mine = own[(*own_at, pl.ds(FEATS, 16), slice(None))].astype(F32)
    n = COMBOS
    there = stats[0:n] + stats[n : 2 * n] + stats[2 * n : 3 * n]
    here = mine[0:n] + mine[n : 2 * n] + mine[2 * n : 3 * n]
    best = jnp.maximum(there, here)
    grow = jnp.exp(there - best)
    total = grow + jnp.exp(here - best)
    share = grow / total
    partner = stats[3 * n : 3 * n + 1] + mine[3 * n : 3 * n + 1]
    blocks = []
    for place in range(COMBOS):
        rows = pl.ds(place * HEAD, HEAD)
        far = came[rows, :].astype(F32)
        near = own[(*own_at, rows, slice(None))].astype(F32)
        blocks.append(near + share[place : place + 1] * (far - near))
    return blocks, best + jnp.log(total), partner


def hop_kernel(step, came, own, out):
    blocks, lse, partner = merged(came, own, (step,))
    for place in range(COMBOS):
        out[pl.ds(place * HEAD, HEAD), :] = blocks[place].astype(BF16)
    out[pl.ds(FEATS, 16), :] = stat_rows(lse, partner)


def last_kernel(*refs):
    came, own, (out, across) = refs[:CHUNKS], refs[CHUNKS : 2 * CHUNKS], refs[2 * CHUNKS :]
    for chunk in range(CHUNKS):
        blocks, _, partner = merged(came[chunk], own[chunk], (LEV - 1,))
        lanes = pl.ds(chunk * CELLS, CELLS)
        for place in range(COMBOS):
            out[pl.ds(place * HEAD, HEAD), lanes] = blocks[place].astype(BF16)
        across[:, lanes] = jnp.broadcast_to(partner, (8, CELLS))


def vmem_call(kernel, out_shape, name, *args, scratch=()):
    vmem = pl.BlockSpec(memory_space=pltpu.VMEM)
    return pl.pallas_call(
        kernel,
        out_shape=out_shape,
        in_specs=[vmem] * len(args),
        out_specs=jax.tree.map(lambda _: vmem, out_shape),
        scratch_shapes=scratch,
        compiler_params=pltpu.CompilerParams(vmem_limit_bytes=VMEM_LIMIT),
        name=name,
    )(*args)


def pole_matrix(across):
    lane = lax.broadcasted_iota(jnp.int32, (1, NLON), 1)
    sector = (lane // SEC + LEV // 2) % LEV
    source = sector * SEC + across[0:1, :].astype(jnp.int32)
    place = lax.broadcasted_iota(jnp.int32, (NLON, NLON), 0)
    return jnp.where(place == source, 1.0, 0.0).astype(BF16)


def area_of(row):
    return math.cos(math.pi * (row + 0.5) / NLAT - math.pi / 2)


def coefficients(row):
    area, polar, inner = area_of(row), area_of(max(row - 1, 0)), area_of(row + 1)
    denom = 3.0 * area + polar + inner
    return area / denom, polar / denom, inner / denom


def edge_kernel(rows, out):
    out[...] = rows[pl.ds((GROUP - HOPS) * (1 - lax.axis_index("half")), HOPS)]


def diffuse_rows(start, low, high, pole, one, two, store):
    readers = (start, lambda row: one[row], lambda row: two[row])
    for step in range(HOPS):
        read = readers[step]
        reach = HOPS - 1 - step
        first = 0 if pole is not None else low - reach
        here = read(first)
        if pole is None:
            before = read(first - 1)
        else:
            top, mid, _ = pieces(here)
            both = jnp.concatenate([top, mid], axis=0).astype(BF16)
            turned = jnp.dot(both, pole, preferred_element_type=F32)
            before = turned[0:8] + turned[8:16]
        for row in range(first, high + reach):
            after = read(row + 1)
            area, polar, inner = coefficients(row)
            beside = pltpu.roll(here, 1, 1) + pltpu.roll(here, NLON - 1, 1)
            state = area * (here + beside) + polar * before + inner * after
            if step == 0:
                one[row] = state
            elif step == 1:
                two[row] = state
            else:
                total = start(row) + one[row] + here + state
                store(row, total * (1.0 / (HOPS + 1.0)))
            before, here = here, after


def inner_kernel(rows, across, out, raw, one, two):
    south = lax.axis_index("half")
    raw[...] = rows[...].astype(F32)

    def place(row):
        return row + south * (GROUP - 1 - 2 * row)

    def store(row, value):
        out[place(row)] = value.astype(BF16)

    pole = pole_matrix(across)
    diffuse_rows(lambda row: raw[place(row)], 0, GROUP - HOPS, pole, one, two, store)


def outer_kernel(rows, halo, inner, out, raw, edge, one, two):
    south = lax.axis_index("half")
    raw[...] = rows[...].astype(F32)
    edge[...] = halo[...].astype(F32)
    out[...] = inner[...]

    def place(row):
        return row + south * (GROUP - 1 - 2 * row)

    def start(row):
        if row < GROUP:
            return raw[place(row)]
        k = row - GROUP
        return edge[k + south * (HOPS - 1 - 2 * k)]

    def store(row, value):
        out[place(row)] = value.astype(BF16)

    diffuse_rows(start, GROUP - HOPS, GROUP, None, one, two, store)


def state_rows(count):
    return pltpu.VMEM((count, 8, NLON), F32)


def project_kernel(parts, weight, out):
    low = jnp.concatenate([parts[block_of(2 * k)] for k in range(LATENTS)], axis=0)
    high = jnp.concatenate([parts[block_of(2 * k + 1)] for k in range(LATENTS)], axis=0)
    summed = jnp.dot(low, weight[0:FEATS], preferred_element_type=F32)
    summed += jnp.dot(high, weight[FEATS:E], preferred_element_type=F32)
    for latent in range(LATENTS):
        rows = slice(latent * SEC, (latent + 1) * SEC)
        out[0, :, pl.ds(latent * E, E)] = summed[rows].astype(BF16)


def body(
    level_tokens, latent_queries, key_weight, value_weight, out_weight, level_valid, pole_partner
):
    tokens = jnp.transpose(level_tokens[0], (1, 0, 2))
    ring = [(RING[i], RING[(i + 1) % LEV]) for i in range(LEV)]
    args = (
        level_valid, latent_queries, key_weight, value_weight, tokens, pole_partner[None]
    )
    message = (ROWS, CELLS)
    *going, values, weights, stats = first_block(*args)
    came = [lax.ppermute(block, "lev", ring) for block in going]
    shapes = (jax.ShapeDtypeStruct((LEV, *message), BF16),) * CHUNKS
    own = vmem_call(blocks_kernel, shapes, "all_blocks", values, weights, stats)
    for step in range(1, LEV - 1):
        merge = functools.partial(hop_kernel, step)
        shape = jax.ShapeDtypeStruct(message, BF16)
        going = [vmem_call(merge, shape, "hop", came[c], own[c]) for c in range(CHUNKS)]
        came = [lax.ppermute(block, "lev", ring) for block in going]
    pooled, across = vmem_call(
        last_kernel,
        (
            jax.ShapeDtypeStruct((FEATS, NLON), BF16),
            jax.ShapeDtypeStruct((8, NLON), F32),
        ),
        "last_hop",
        *came,
        *own,
    )

    rows = pooled.reshape(GROUP, FEATS // GROUP, NLON)
    rows = lax.all_to_all(rows, "row", split_axis=0, concat_axis=0, tiled=True)
    shape = jax.ShapeDtypeStruct((HOPS, *rows.shape[1:]), BF16)
    edge = vmem_call(edge_kernel, shape, "edge", rows)
    turned = [(lev, LEV + (lev + LEV // 2) % LEV) for lev in range(LEV)]
    turned += [(there, here) for here, there in turned]
    halo = lax.ppermute(edge, ("half", "lev"), turned)
    shape = jax.ShapeDtypeStruct(rows.shape, BF16)
    states = [state_rows(GROUP), state_rows(GROUP + HOPS), state_rows(GROUP + HOPS)]
    mean = vmem_call(inner_kernel, shape, "diffuse_inner", rows, across, scratch=states)
    states.insert(1, state_rows(HOPS))
    mean = vmem_call(outer_kernel, shape, "diffuse_outer", rows, halo, mean, scratch=states)
    mean = lax.all_to_all(mean, "row", split_axis=0, concat_axis=0, tiled=True)
    sectors = mean.reshape(FEATS, NLON).T.reshape(LEV, SEC, FEATS)
    parts = lax.all_to_all(sectors, "lev", split_axis=0, concat_axis=0, tiled=True)
    shape = jax.ShapeDtypeStruct((1, SEC, LATENTS * E), BF16)
    return vmem_call(project_kernel, shape, "project", parts, out_weight)


def solution(mesh):
    halves = mesh.shape["lat"] // GROUP
    devices = mesh.devices.reshape(halves, GROUP, mesh.shape["lev"])
    mesh = Mesh(devices, ("half", "row", "lev"))
    lat = ("half", "row")
    in_specs = (P(lat, None, "lev", None), P(), P(), P(), P(), P(), P("lev"))
    out_specs = P(lat, "lev", None)
    return jax.shard_map(body, mesh=mesh, in_specs=in_specs, out_specs=out_specs, check_vma=False)
```

```python
import functools
import math

import jax
import jax.numpy as jnp
from jax import lax
from jax.experimental import pallas as pl
from jax.experimental.pallas import tpu as pltpu
from jax.sharding import Mesh
from jax.sharding import PartitionSpec as P

HEADS = 8
LATENTS = 4
HOPS = 3
E = 512
HEAD = E // HEADS
NLAT = 64
NLON = 512
LEV = 8
SEC = NLON // LEV
LEV_DEV = 5
GROUP = 32
FEATS = LATENTS * E // LEV
COMBOS = FEATS // HEAD
ROWS = FEATS + 16
RING = (0, 2, 4, 6, 7, 5, 3, 1)
CHUNKS = 2
CELLS = NLON // CHUNKS
F32 = jnp.float32
BF16 = jnp.bfloat16
NT = (((1,), (1,)), ((), ()))
VMEM_LIMIT = 8 * 1024 * 1024
LEVEL_LIMIT = 24 * 1024 * 1024


def pieces(x):
    high = x.astype(BF16).astype(F32)
    rest = x - high
    mid = rest.astype(BF16).astype(F32)
    return high, mid, rest - mid


def stat_rows(lse, partner):
    high, mid, low = pieces(lse)
    empty = jnp.zeros((16 - 3 * COMBOS - 1, lse.shape[1]), F32)
    return jnp.concatenate([high, mid, low, partner, empty], axis=0).astype(BF16)


def block_of(lev):
    return (lev + lax.axis_index("half") * (LEV // 2)) % LEV


def ring_place(lev):
    return jnp.where(lev % 2 == 0, lev // 2, (2 * LEV - 1 - lev) // 2)


def grouped_softmax(scores, valid, lev):
    kept = [valid[lev * LEV_DEV + level] == 1 for level in range(LEV_DEV)]
    masked = [jnp.where(keep, score, -1e30) for keep, score in zip(kept, scores)]
    top = functools.reduce(jnp.maximum, masked)
    expo = [jnp.where(keep, jnp.exp(score - top), 0.0) for keep, score in zip(kept, masked)]
    total = functools.reduce(jnp.add, expo)
    return [part / total for part in expo], top + jnp.log(total)


def partner_row(partner, lev):
    lane = lax.broadcasted_iota(jnp.int32, (SEC, NLON), 1)
    same = lane % SEC == lax.broadcasted_iota(jnp.int32, (SEC, NLON), 0)
    same = jnp.logical_and(same, lane // SEC == lev)
    local = jnp.broadcast_to((partner[...] % SEC).astype(F32), (8, SEC)).astype(BF16)
    spread = jnp.where(same, 1.0, 0.0).astype(BF16)
    return jnp.dot(local, spread, preferred_element_type=F32)[0:1]


def head_rows(query, latent_rows):
    width = query.shape[1]
    lane_head = lax.broadcasted_iota(jnp.int32, (HEADS, width), 1) // HEAD
    own_head = lane_head == lax.broadcasted_iota(jnp.int32, (HEADS, width), 0)
    rows = [jnp.where(own_head, row, 0.0) for row in latent_rows]
    return jnp.concatenate(rows, axis=0).astype(BF16)


def score_of(spread, block, key_weight):
    keys = jnp.dot(block, key_weight[...], preferred_element_type=F32).astype(BF16)
    score = lax.dot_general(spread, keys, NT, preferred_element_type=F32)
    return score * (1.0 / math.sqrt(HEAD))


def first_kernel(
    valid_at, query_at, key_at, value_at, tokens_at, partner_at,
    first, second, values, weights, stats,
    valid, query, key_weight, value_weight, tokens, partner, sems,
):
    lev = lax.axis_index("lev")
    copies = [
        pltpu.make_async_copy(key_at, key_weight, sems.at[0]),
        pltpu.make_async_copy(value_at, value_weight, sems.at[1]),
        pltpu.make_async_copy(query_at, query, sems.at[2]),
        pltpu.make_async_copy(valid_at, valid, sems.at[3]),
        pltpu.make_async_copy(partner_at, partner, sems.at[4]),
    ]
    fetches = [
        pltpu.make_async_copy(tokens_at.at[level], tokens.at[level], sems.at[5 + level])
        for level in range(LEV_DEV)
    ]
    for copy in copies + fetches:
        copy.start()
    for copy in copies:
        copy.wait()
    rows = query[...].astype(F32)
    spread = head_rows(query, [rows[k : k + 1] for k in range(LATENTS)])
    value_t = value_weight[...].astype(F32).T.astype(BF16)
    scores = []
    for level in range(LEV_DEV):
        fetches[level].wait()
        here = tokens[level]
        scores.append(score_of(spread, here, key_weight))
        value = lax.dot_general(value_t, here, NT, preferred_element_type=F32)
        values[level] = value.astype(BF16).astype(F32)
    shares, lse = grouped_softmax(scores, valid, lev)
    for level in range(LEV_DEV):
        weights[level] = shares[level]
    across = partner_row(partner, lev)
    for block in range(LEV):
        stats[block] = stat_rows(lse[block * COMBOS : (block + 1) * COMBOS], across)

    place = (ring_place(lev) + LEV // 2) % LEV
    block = block_of(jnp.where(place < LEV // 2, 2 * place, 2 * LEV - 1 - 2 * place))
    for chunk, out in enumerate((first, second)):
        lanes = pl.ds(chunk * CELLS, CELLS)
        for place in range(COMBOS):
            head = pl.multiple_of((block % 2 * COMBOS + place) * HEAD, HEAD)
            row = pl.ds(block * COMBOS + place, 1)
            terms = [
                weights[level, row, lanes] * values[level, pl.ds(head, HEAD), lanes]
                for level in range(LEV_DEV)
            ]
            summed = functools.reduce(jnp.add, terms)
            out[pl.ds(place * HEAD, HEAD), :] = summed.astype(BF16)
        out[pl.ds(FEATS, 16), :] = stats[block, :, lanes]


def first_block(*args):
    hbm = pl.BlockSpec(memory_space=pltpu.HBM)
    vmem = pl.BlockSpec(memory_space=pltpu.VMEM)
    return pl.pallas_call(
        first_kernel,
        out_shape=(
            jax.ShapeDtypeStruct((ROWS, CELLS), BF16),
            jax.ShapeDtypeStruct((ROWS, CELLS), BF16),
            jax.ShapeDtypeStruct((LEV_DEV, E, NLON), F32),
            jax.ShapeDtypeStruct((LEV_DEV, LATENTS * HEADS, NLON), F32),
            jax.ShapeDtypeStruct((LEV, 16, NLON), BF16),
        ),
        in_specs=[hbm] * len(args),
        out_specs=(vmem,) * 5,
        scratch_shapes=[
            pltpu.SMEM((LEV * LEV_DEV,), jnp.int32),
            pltpu.VMEM((LATENTS, E), BF16),
            pltpu.VMEM((E, E), BF16),
            pltpu.VMEM((E, E), BF16),
            pltpu.VMEM((LEV_DEV, NLON, E), BF16),
            pltpu.VMEM((1, SEC), jnp.int32),
            pltpu.SemaphoreType.DMA((5 + LEV_DEV,)),
        ],
        compiler_params=pltpu.CompilerParams(vmem_limit_bytes=LEVEL_LIMIT),
        name="first_block",
    )(*[pltpu.with_memory_space_constraint(arg, pltpu.HBM) for arg in args])


def ring_slot(ahead):
    slot = jnp.where(ahead <= LEV // 2, LEV // 2 - ahead, ahead - 1)
    return jnp.where(ahead == 0, LEV - 1, slot)


def blocks_kernel(values, weights, stats, own, other, backward, backward_other):
    here = ring_place(lax.axis_index("lev"))
    slots = [
        ring_slot((ring_place(block_of(block)) + LEV - here) % LEV) for block in range(LEV)
    ]
    for head in range(HEADS):
        for lane in range(0, NLON, 128):
            lanes = pl.ds(lane, 128)
            terms = [
                values[level, pl.ds(head * HEAD, HEAD), lanes] for level in range(LEV_DEV)
            ]
            for latent in range(LATENTS):
                row = pl.ds(latent * HEADS + head, 1)
                summed = weights[0, row, lanes] * terms[0]
                for level in range(1, LEV_DEV):
                    summed = summed + weights[level, row, lanes] * terms[level]
                block, place = divmod(latent * HEADS + head, COMBOS)
                out = (own, other)[lane // CELLS]
                lanes_out = pl.ds(lane % CELLS, 128)
                out[slots[block], pl.ds(place * HEAD, HEAD), lanes_out] = summed.astype(BF16)
    for block in range(LEV):
        for chunk, out in enumerate((own, other)):
            lanes = pl.ds(chunk * CELLS, CELLS)
            out[slots[block], pl.ds(FEATS, 16), :] = stats[block, :, lanes]
    backward[...] = own[LEV // 2]
    backward_other[...] = other[LEV // 2]


def merged(*messages):
    stats = [message[pl.ds(FEATS, 16), :].astype(F32) for message in messages]
    n = COMBOS
    lses = [rows[0:n] + rows[n : 2 * n] + rows[2 * n : 3 * n] for rows in stats]
    best = functools.reduce(jnp.maximum, lses)
    grown = [jnp.exp(lse - best) for lse in lses]
    total = functools.reduce(jnp.add, grown)
    shares = [part / total for part in grown]
    partner = functools.reduce(jnp.add, [rows[3 * n : 3 * n + 1] for rows in stats])
    blocks = []
    for place in range(COMBOS):
        rows = pl.ds(place * HEAD, HEAD)
        terms = [
            share[place : place + 1] * message[rows, :].astype(F32)
            for share, message in zip(shares, messages)
        ]
        blocks.append(functools.reduce(jnp.add, terms))
    return blocks, best + jnp.log(total), partner


def hop_kernel(slot, came, own, out):
    blocks, lse, partner = merged(came, own.at[slot])
    for place in range(COMBOS):
        out[pl.ds(place * HEAD, HEAD), :] = blocks[place].astype(BF16)
    out[pl.ds(FEATS, 16), :] = stat_rows(lse, partner)


def last_kernel(*refs):
    forward, backward, own = (refs[i * CHUNKS : (i + 1) * CHUNKS] for i in range(3))
    out, across = refs[3 * CHUNKS :]
    for chunk in range(CHUNKS):
        blocks, _, partner = merged(forward[chunk], backward[chunk], own[chunk].at[LEV - 1])
        lanes = pl.ds(chunk * CELLS, CELLS)
        for place in range(COMBOS):
            out[pl.ds(place * HEAD, HEAD), lanes] = blocks[place].astype(BF16)
        across[:, lanes] = jnp.broadcast_to(partner, (8, CELLS))


def vmem_call(kernel, out_shape, name, *args, scratch=()):
    vmem = pl.BlockSpec(memory_space=pltpu.VMEM)
    return pl.pallas_call(
        kernel,
        out_shape=out_shape,
        in_specs=[vmem] * len(args),
        out_specs=jax.tree.map(lambda _: vmem, out_shape),
        scratch_shapes=scratch,
        compiler_params=pltpu.CompilerParams(vmem_limit_bytes=VMEM_LIMIT),
        name=name,
    )(*args)


def pole_matrix(across):
    lane = lax.broadcasted_iota(jnp.int32, (1, NLON), 1)
    sector = (lane // SEC + LEV // 2) % LEV
    source = sector * SEC + across[0:1, :].astype(jnp.int32)
    place = lax.broadcasted_iota(jnp.int32, (NLON, NLON), 0)
    return jnp.where(place == source, 1.0, 0.0).astype(BF16)


def area_of(row):
    return math.cos(math.pi * (row + 0.5) / NLAT - math.pi / 2)


def coefficients(row):
    area, polar, inner = area_of(row), area_of(max(row - 1, 0)), area_of(row + 1)
    denom = 3.0 * area + polar + inner
    return area / denom, polar / denom, inner / denom


def edge_kernel(rows, out):
    out[...] = rows[pl.ds((GROUP - HOPS) * (1 - lax.axis_index("half")), HOPS)]


def diffuse_rows(start, low, high, pole, one, two, store):
    readers = (start, lambda row: one[row], lambda row: two[row])
    for step in range(HOPS):
        read = readers[step]
        reach = HOPS - 1 - step
        first = 0 if pole is not None else low - reach
        here = read(first)
        if pole is None:
            before = read(first - 1)
        else:
            top, mid, _ = pieces(here)
            both = jnp.concatenate([top, mid], axis=0).astype(BF16)
            turned = jnp.dot(both, pole, preferred_element_type=F32)
            before = turned[0:8] + turned[8:16]
        for row in range(first, high + reach):
            after = read(row + 1)
            area, polar, inner = coefficients(row)
            beside = pltpu.roll(here, 1, 1) + pltpu.roll(here, NLON - 1, 1)
            state = area * (here + beside) + polar * before + inner * after
            if step == 0:
                one[row] = state
            elif step == 1:
                two[row] = state
            else:
                total = start(row) + one[row] + here + state
                store(row, total * (1.0 / (HOPS + 1.0)))
            before, here = here, after


def inner_kernel(rows, across, out, raw, one, two):
    south = lax.axis_index("half")
    raw[...] = rows[...].astype(F32)

    def place(row):
        return row + south * (GROUP - 1 - 2 * row)

    def store(row, value):
        out[place(row)] = value.astype(BF16)

    pole = pole_matrix(across)
    diffuse_rows(lambda row: raw[place(row)], 0, GROUP - HOPS, pole, one, two, store)


def outer_kernel(rows, halo, inner, out, raw, edge, one, two):
    south = lax.axis_index("half")
    raw[...] = rows[...].astype(F32)
    edge[...] = halo[...].astype(F32)
    out[...] = inner[...]

    def place(row):
        return row + south * (GROUP - 1 - 2 * row)

    def start(row):
        if row < GROUP:
            return raw[place(row)]
        k = row - GROUP
        return edge[k + south * (HOPS - 1 - 2 * k)]

    def store(row, value):
        out[place(row)] = value.astype(BF16)

    diffuse_rows(start, GROUP - HOPS, GROUP, None, one, two, store)


def state_rows(count):
    return pltpu.VMEM((count, 8, NLON), F32)


def project_kernel(parts, weight, out):
    low = jnp.concatenate([parts[block_of(2 * k)] for k in range(LATENTS)], axis=0)
    high = jnp.concatenate([parts[block_of(2 * k + 1)] for k in range(LATENTS)], axis=0)
    summed = jnp.dot(low, weight[0:FEATS], preferred_element_type=F32)
    summed += jnp.dot(high, weight[FEATS:E], preferred_element_type=F32)
    for latent in range(LATENTS):
        rows = slice(latent * SEC, (latent + 1) * SEC)
        out[0, :, pl.ds(latent * E, E)] = summed[rows].astype(BF16)


def body(
    level_tokens, latent_queries, key_weight, value_weight, out_weight, level_valid, pole_partner
):
    tokens = jnp.transpose(level_tokens[0], (1, 0, 2))
    ring = [(RING[i], RING[(i + 1) % LEV]) for i in range(LEV)]
    args = (
        level_valid, latent_queries, key_weight, value_weight, tokens, pole_partner[None]
    )
    message = (ROWS, CELLS)
    *forward, values, weights, stats = first_block(*args)
    block = jax.ShapeDtypeStruct(message, BF16)
    shapes = (jax.ShapeDtypeStruct((LEV, *message), BF16),) * CHUNKS + (block,) * CHUNKS
    blocks = vmem_call(blocks_kernel, shapes, "all_blocks", values, weights, stats)
    own, backward = blocks[:CHUNKS], list(blocks[CHUNKS:])
    back = [(there, here) for here, there in ring]
    for step in range(LEV // 2):
        for chunk in range(CHUNKS):
            came = lax.ppermute(forward[chunk], "lev", ring)
            if step < LEV // 2 - 1:
                merge = functools.partial(hop_kernel, step + 1)
                came = vmem_call(merge, block, "hop", came, own[chunk])
            forward[chunk] = came
            if step == LEV // 2 - 1:
                continue
            came = lax.ppermute(backward[chunk], "lev", back)
            if step < LEV // 2 - 2:
                merge = functools.partial(hop_kernel, LEV // 2 + step + 1)
                came = vmem_call(merge, block, "hop", came, own[chunk])
            backward[chunk] = came
    pooled, across = vmem_call(
        last_kernel,
        (
            jax.ShapeDtypeStruct((FEATS, NLON), BF16),
            jax.ShapeDtypeStruct((8, NLON), F32),
        ),
        "last_hop",
        *forward,
        *backward,
        *own,
    )

    rows = pooled.reshape(GROUP, FEATS // GROUP, NLON)
    rows = lax.all_to_all(rows, "row", split_axis=0, concat_axis=0, tiled=True)
    shape = jax.ShapeDtypeStruct((HOPS, *rows.shape[1:]), BF16)
    edge = vmem_call(edge_kernel, shape, "edge", rows)
    turned = [(lev, LEV + (lev + LEV // 2) % LEV) for lev in range(LEV)]
    turned += [(there, here) for here, there in turned]
    halo = lax.ppermute(edge, ("half", "lev"), turned)
    shape = jax.ShapeDtypeStruct(rows.shape, BF16)
    states = [state_rows(GROUP), state_rows(GROUP + HOPS), state_rows(GROUP + HOPS)]
    mean = vmem_call(inner_kernel, shape, "diffuse_inner", rows, across, scratch=states)
    states.insert(1, state_rows(HOPS))
    mean = vmem_call(outer_kernel, shape, "diffuse_outer", rows, halo, mean, scratch=states)
    mean = lax.all_to_all(mean, "row", split_axis=0, concat_axis=0, tiled=True)
    sectors = mean.reshape(FEATS, NLON).T.reshape(LEV, SEC, FEATS)
    parts = lax.all_to_all(sectors, "lev", split_axis=0, concat_axis=0, tiled=True)
    shape = jax.ShapeDtypeStruct((1, SEC, LATENTS * E), BF16)
    return vmem_call(project_kernel, shape, "project", parts, out_weight)


def solution(mesh):
    halves = mesh.shape["lat"] // GROUP
    devices = mesh.devices.reshape(halves, GROUP, mesh.shape["lev"])
    mesh = Mesh(devices, ("half", "row", "lev"))
    lat = ("half", "row")
    in_specs = (P(lat, None, "lev", None), P(), P(), P(), P(), P(), P("lev"))
    out_specs = P(lat, "lev", None)
    return jax.shard_map(body, mesh=mesh, in_specs=in_specs, out_specs=out_specs, check_vma=False)
```

```python
import functools
import math

import jax
import jax.numpy as jnp
from jax import lax
from jax.experimental import pallas as pl
from jax.experimental.pallas import tpu as pltpu
from jax.sharding import Mesh
from jax.sharding import PartitionSpec as P

HEADS = 8
LATENTS = 4
HOPS = 3
E = 512
HEAD = E // HEADS
NLAT = 64
NLON = 512
LEV = 8
SEC = NLON // LEV
LEV_DEV = 5
GROUP = 32
FEATS = LATENTS * E // LEV
COMBOS = FEATS // HEAD
ROWS = FEATS + 16
RING = (0, 2, 4, 6, 7, 5, 3, 1)
CHUNKS = 2
CELLS = NLON // CHUNKS
F32 = jnp.float32
BF16 = jnp.bfloat16
NT = (((1,), (1,)), ((), ()))
VMEM_LIMIT = 8 * 1024 * 1024
LEVEL_LIMIT = 24 * 1024 * 1024


def pieces(x):
    high = x.astype(BF16).astype(F32)
    rest = x - high
    mid = rest.astype(BF16).astype(F32)
    return high, mid, rest - mid


def stat_rows(lse, partner):
    high, mid, low = pieces(lse)
    empty = jnp.zeros((16 - 3 * COMBOS - 1, lse.shape[1]), F32)
    return jnp.concatenate([high, mid, low, partner, empty], axis=0).astype(BF16)


def block_of(lev):
    return (lev + lax.axis_index("half") * (LEV // 2)) % LEV


def ring_place(lev):
    return jnp.where(lev % 2 == 0, lev // 2, (2 * LEV - 1 - lev) // 2)


def grouped_softmax(scores, valid, lev):
    kept = [valid[lev * LEV_DEV + level] == 1 for level in range(LEV_DEV)]
    masked = [jnp.where(keep, score, -1e30) for keep, score in zip(kept, scores)]
    top = functools.reduce(jnp.maximum, masked)
    expo = [jnp.where(keep, jnp.exp(score - top), 0.0) for keep, score in zip(kept, masked)]
    total = functools.reduce(jnp.add, expo)
    return [part / total for part in expo], top + jnp.log(total)


def partner_row(partner, lev):
    lane = lax.broadcasted_iota(jnp.int32, (SEC, NLON), 1)
    same = lane % SEC == lax.broadcasted_iota(jnp.int32, (SEC, NLON), 0)
    same = jnp.logical_and(same, lane // SEC == lev)
    local = jnp.broadcast_to((partner[...] % SEC).astype(F32), (8, SEC)).astype(BF16)
    spread = jnp.where(same, 1.0, 0.0).astype(BF16)
    return jnp.dot(local, spread, preferred_element_type=F32)[0:1]


def head_rows(query, latent_rows):
    width = query.shape[1]
    lane_head = lax.broadcasted_iota(jnp.int32, (HEADS, width), 1) // HEAD
    own_head = lane_head == lax.broadcasted_iota(jnp.int32, (HEADS, width), 0)
    rows = [jnp.where(own_head, row, 0.0) for row in latent_rows]
    return jnp.concatenate(rows, axis=0).astype(BF16)


def score_of(spread, block, key_weight):
    keys = jnp.dot(block, key_weight[...], preferred_element_type=F32).astype(BF16)
    score = lax.dot_general(spread, keys, NT, preferred_element_type=F32)
    return score * (1.0 / math.sqrt(HEAD))


def first_kernel(
    valid_at, query_at, key_at, value_at, tokens_at, partner_at,
    first, second, values, weights, stats,
    valid, query, key_weight, value_weight, tokens, partner, sems,
):
    lev = lax.axis_index("lev")
    copies = [
        pltpu.make_async_copy(key_at, key_weight, sems.at[0]),
        pltpu.make_async_copy(value_at, value_weight, sems.at[1]),
        pltpu.make_async_copy(query_at, query, sems.at[2]),
        pltpu.make_async_copy(valid_at, valid, sems.at[3]),
        pltpu.make_async_copy(partner_at, partner, sems.at[4]),
    ]
    fetches = [
        pltpu.make_async_copy(tokens_at.at[level], tokens.at[level], sems.at[5 + level])
        for level in range(LEV_DEV)
    ]
    for copy in copies + fetches:
        copy.start()
    for copy in copies:
        copy.wait()
    rows = query[...].astype(F32)
    spread = head_rows(query, [rows[k : k + 1] for k in range(LATENTS)])
    value_t = value_weight[...].astype(F32).T.astype(BF16)
    scores = []
    for level in range(LEV_DEV):
        fetches[level].wait()
        here = tokens[level]
        scores.append(score_of(spread, here, key_weight))
        value = lax.dot_general(value_t, here, NT, preferred_element_type=F32)
        values[level] = value.astype(BF16).astype(F32)
    shares, lse = grouped_softmax(scores, valid, lev)
    for level in range(LEV_DEV):
        weights[level] = shares[level]
    across = partner_row(partner, lev)
    for block in range(LEV):
        stats[block] = stat_rows(lse[block * COMBOS : (block + 1) * COMBOS], across)

    for ahead, out in ((LEV // 2, first), (LEV // 2 + 1, second)):
        place = (ring_place(lev) + ahead) % LEV
        block = block_of(jnp.where(place < LEV // 2, 2 * place, 2 * LEV - 1 - 2 * place))
        for place in range(COMBOS):
            head = pl.multiple_of((block % 2 * COMBOS + place) * HEAD, HEAD)
            row = pl.ds(block * COMBOS + place, 1)
            terms = [
                weights[level, row, :] * values[level, pl.ds(head, HEAD), :]
                for level in range(LEV_DEV)
            ]
            summed = functools.reduce(jnp.add, terms)
            out[pl.ds(place * HEAD, HEAD), :] = summed.astype(BF16)
        out[pl.ds(FEATS, 16), :] = stats[block]


def first_block(*args):
    hbm = pl.BlockSpec(memory_space=pltpu.HBM)
    vmem = pl.BlockSpec(memory_space=pltpu.VMEM)
    return pl.pallas_call(
        first_kernel,
        out_shape=(
            jax.ShapeDtypeStruct((ROWS, NLON), BF16),
            jax.ShapeDtypeStruct((ROWS, NLON), BF16),
            jax.ShapeDtypeStruct((LEV_DEV, E, NLON), F32),
            jax.ShapeDtypeStruct((LEV_DEV, LATENTS * HEADS, NLON), F32),
            jax.ShapeDtypeStruct((LEV, 16, NLON), BF16),
        ),
        in_specs=[hbm] * len(args),
        out_specs=(vmem,) * 5,
        scratch_shapes=[
            pltpu.SMEM((LEV * LEV_DEV,), jnp.int32),
            pltpu.VMEM((LATENTS, E), BF16),
            pltpu.VMEM((E, E), BF16),
            pltpu.VMEM((E, E), BF16),
            pltpu.VMEM((LEV_DEV, NLON, E), BF16),
            pltpu.VMEM((1, SEC), jnp.int32),
            pltpu.SemaphoreType.DMA((5 + LEV_DEV,)),
        ],
        compiler_params=pltpu.CompilerParams(vmem_limit_bytes=LEVEL_LIMIT),
        name="first_block",
    )(*[pltpu.with_memory_space_constraint(arg, pltpu.HBM) for arg in args])


def ring_slot(ahead):
    slot = jnp.where(ahead <= LEV // 2, LEV // 2 - ahead, ahead - 1)
    return jnp.where(ahead == 0, LEV - 1, slot)


def blocks_kernel(values, weights, stats, own):
    here = ring_place(lax.axis_index("lev"))
    slots = [
        ring_slot((ring_place(block_of(block)) + LEV - here) % LEV) for block in range(LEV)
    ]
    for head in range(HEADS):
        for lane in range(0, NLON, 128):
            lanes = pl.ds(lane, 128)
            terms = [
                values[level, pl.ds(head * HEAD, HEAD), lanes] for level in range(LEV_DEV)
            ]
            for latent in range(LATENTS):
                row = pl.ds(latent * HEADS + head, 1)
                summed = weights[0, row, lanes] * terms[0]
                for level in range(1, LEV_DEV):
                    summed = summed + weights[level, row, lanes] * terms[level]
                block, place = divmod(latent * HEADS + head, COMBOS)
                own[slots[block], pl.ds(place * HEAD, HEAD), lanes] = summed.astype(BF16)
    for block in range(LEV):
        own[slots[block], pl.ds(FEATS, 16), :] = stats[block]


def merged(*messages):
    stats = [message[pl.ds(FEATS, 16), :].astype(F32) for message in messages]
    n = COMBOS
    lses = [rows[0:n] + rows[n : 2 * n] + rows[2 * n : 3 * n] for rows in stats]
    best = functools.reduce(jnp.maximum, lses)
    grown = [jnp.exp(lse - best) for lse in lses]
    total = functools.reduce(jnp.add, grown)
    shares = [part / total for part in grown]
    partner = functools.reduce(jnp.add, [rows[3 * n : 3 * n + 1] for rows in stats])
    blocks = []
    for place in range(COMBOS):
        rows = pl.ds(place * HEAD, HEAD)
        terms = [
            share[place : place + 1] * message[rows, :].astype(F32)
            for share, message in zip(shares, messages)
        ]
        blocks.append(functools.reduce(jnp.add, terms))
    return blocks, best + jnp.log(total), partner


def lanes_of(chunk):
    return pl.ds(chunk * CELLS, CELLS)


def hop_kernel(slot, came_lanes, lanes, came, own, out):
    blocks, lse, partner = merged(came.at[:, came_lanes], own.at[slot, :, lanes])
    for place in range(COMBOS):
        out[pl.ds(place * HEAD, HEAD), :] = blocks[place].astype(BF16)
    out[pl.ds(FEATS, 16), :] = stat_rows(lse, partner)


def last_kernel(*refs):
    forward, (backward, own, out, across) = refs[:CHUNKS], refs[CHUNKS:]
    for chunk in range(CHUNKS):
        lanes = lanes_of(chunk)
        blocks, _, partner = merged(
            forward[chunk], backward.at[:, lanes], own.at[LEV - 1, :, lanes]
        )
        for place in range(COMBOS):
            out[pl.ds(place * HEAD, HEAD), lanes] = blocks[place].astype(BF16)
        across[:, lanes] = jnp.broadcast_to(partner, (8, CELLS))


def vmem_call(kernel, out_shape, name, *args, scratch=()):
    vmem = pl.BlockSpec(memory_space=pltpu.VMEM)
    return pl.pallas_call(
        kernel,
        out_shape=out_shape,
        in_specs=[vmem] * len(args),
        out_specs=jax.tree.map(lambda _: vmem, out_shape),
        scratch_shapes=scratch,
        compiler_params=pltpu.CompilerParams(vmem_limit_bytes=VMEM_LIMIT),
        name=name,
    )(*args)


def pole_matrix(across):
    lane = lax.broadcasted_iota(jnp.int32, (1, NLON), 1)
    sector = (lane // SEC + LEV // 2) % LEV
    source = sector * SEC + across[0:1, :].astype(jnp.int32)
    place = lax.broadcasted_iota(jnp.int32, (NLON, NLON), 0)
    return jnp.where(place == source, 1.0, 0.0).astype(BF16)


def area_of(row):
    return math.cos(math.pi * (row + 0.5) / NLAT - math.pi / 2)


def coefficients(row):
    area, polar, inner = area_of(row), area_of(max(row - 1, 0)), area_of(row + 1)
    denom = 3.0 * area + polar + inner
    return area / denom, polar / denom, inner / denom


def edge_kernel(rows, out):
    out[...] = rows[pl.ds((GROUP - HOPS) * (1 - lax.axis_index("half")), HOPS)]


def diffuse_rows(start, low, high, pole, one, two, store):
    readers = (start, lambda row: one[row], lambda row: two[row])
    for step in range(HOPS):
        read = readers[step]
        reach = HOPS - 1 - step
        first = 0 if pole is not None else low - reach
        here = read(first)
        if pole is None:
            before = read(first - 1)
        else:
            top, mid, _ = pieces(here)
            both = jnp.concatenate([top, mid], axis=0).astype(BF16)
            turned = jnp.dot(both, pole, preferred_element_type=F32)
            before = turned[0:8] + turned[8:16]
        for row in range(first, high + reach):
            after = read(row + 1)
            area, polar, inner = coefficients(row)
            beside = pltpu.roll(here, 1, 1) + pltpu.roll(here, NLON - 1, 1)
            state = area * (here + beside) + polar * before + inner * after
            if step == 0:
                one[row] = state
            elif step == 1:
                two[row] = state
            else:
                total = start(row) + one[row] + here + state
                store(row, total * (1.0 / (HOPS + 1.0)))
            before, here = here, after


def inner_kernel(rows, across, out, raw, one, two):
    south = lax.axis_index("half")
    raw[...] = rows[...].astype(F32)

    def place(row):
        return row + south * (GROUP - 1 - 2 * row)

    def store(row, value):
        out[place(row)] = value.astype(BF16)

    pole = pole_matrix(across)
    diffuse_rows(lambda row: raw[place(row)], 0, GROUP - HOPS, pole, one, two, store)


def outer_kernel(rows, halo, inner, out, raw, edge, one, two):
    south = lax.axis_index("half")
    raw[...] = rows[...].astype(F32)
    edge[...] = halo[...].astype(F32)
    out[...] = inner[...]

    def place(row):
        return row + south * (GROUP - 1 - 2 * row)

    def start(row):
        if row < GROUP:
            return raw[place(row)]
        k = row - GROUP
        return edge[k + south * (HOPS - 1 - 2 * k)]

    def store(row, value):
        out[place(row)] = value.astype(BF16)

    diffuse_rows(start, GROUP - HOPS, GROUP, None, one, two, store)


def state_rows(count):
    return pltpu.VMEM((count, 8, NLON), F32)


def project_kernel(parts, weight, out):
    low = jnp.concatenate([parts[block_of(2 * k)] for k in range(LATENTS)], axis=0)
    high = jnp.concatenate([parts[block_of(2 * k + 1)] for k in range(LATENTS)], axis=0)
    summed = jnp.dot(low, weight[0:FEATS], preferred_element_type=F32)
    summed += jnp.dot(high, weight[FEATS:E], preferred_element_type=F32)
    for latent in range(LATENTS):
        rows = slice(latent * SEC, (latent + 1) * SEC)
        out[0, :, pl.ds(latent * E, E)] = summed[rows].astype(BF16)


def body(
    level_tokens, latent_queries, key_weight, value_weight, out_weight, level_valid, pole_partner
):
    tokens = jnp.transpose(level_tokens[0], (1, 0, 2))
    ring = [(RING[i], RING[(i + 1) % LEV]) for i in range(LEV)]
    args = (
        level_valid, latent_queries, key_weight, value_weight, tokens, pole_partner[None]
    )
    forward, backward, values, weights, stats = first_block(*args)
    forward = [lax.ppermute(forward, "lev", ring)] * CHUNKS
    whole = jax.ShapeDtypeStruct((ROWS, NLON), BF16)
    part = jax.ShapeDtypeStruct((ROWS, CELLS), BF16)
    shape = jax.ShapeDtypeStruct((LEV, *whole.shape), BF16)
    own = vmem_call(blocks_kernel, shape, "all_blocks", values, weights, stats)
    back = [(there, here) for here, there in ring]
    everything = slice(None)
    for step in range(1, LEV // 2):
        backward = lax.ppermute(backward, "lev", back)
        for chunk in range(CHUNKS):
            lanes = lanes_of(chunk)
            merge = functools.partial(
                hop_kernel, step, lanes if step == 1 else everything, lanes
            )
            going = vmem_call(merge, part, "hop", forward[chunk], own)
            forward[chunk] = lax.ppermute(going, "lev", ring)
        if step < LEV // 2 - 1:
            merge = functools.partial(hop_kernel, LEV // 2 + step, everything, everything)
            backward = vmem_call(merge, whole, "hop", backward, own)
    pooled, across = vmem_call(
        last_kernel,
        (
            jax.ShapeDtypeStruct((FEATS, NLON), BF16),
            jax.ShapeDtypeStruct((8, NLON), F32),
        ),
        "last_hop",
        *forward,
        backward,
        own,
    )

    rows = pooled.reshape(GROUP, FEATS // GROUP, NLON)
    rows = lax.all_to_all(rows, "row", split_axis=0, concat_axis=0, tiled=True)
    shape = jax.ShapeDtypeStruct((HOPS, *rows.shape[1:]), BF16)
    edge = vmem_call(edge_kernel, shape, "edge", rows)
    turned = [(lev, LEV + (lev + LEV // 2) % LEV) for lev in range(LEV)]
    turned += [(there, here) for here, there in turned]
    halo = lax.ppermute(edge, ("half", "lev"), turned)
    shape = jax.ShapeDtypeStruct(rows.shape, BF16)
    states = [state_rows(GROUP), state_rows(GROUP + HOPS), state_rows(GROUP + HOPS)]
    mean = vmem_call(inner_kernel, shape, "diffuse_inner", rows, across, scratch=states)
    states.insert(1, state_rows(HOPS))
    mean = vmem_call(outer_kernel, shape, "diffuse_outer", rows, halo, mean, scratch=states)
    mean = lax.all_to_all(mean, "row", split_axis=0, concat_axis=0, tiled=True)
    sectors = mean.reshape(FEATS, NLON).T.reshape(LEV, SEC, FEATS)
    parts = lax.all_to_all(sectors, "lev", split_axis=0, concat_axis=0, tiled=True)
    shape = jax.ShapeDtypeStruct((1, SEC, LATENTS * E), BF16)
    return vmem_call(project_kernel, shape, "project", parts, out_weight)


def solution(mesh):
    halves = mesh.shape["lat"] // GROUP
    devices = mesh.devices.reshape(halves, GROUP, mesh.shape["lev"])
    mesh = Mesh(devices, ("half", "row", "lev"))
    lat = ("half", "row")
    in_specs = (P(lat, None, "lev", None), P(), P(), P(), P(), P(), P("lev"))
    out_specs = P(lat, "lev", None)
    return jax.shard_map(body, mesh=mesh, in_specs=in_specs, out_specs=out_specs, check_vma=False)
```

```python
import functools
import math

import jax
import jax.numpy as jnp
from jax import lax
from jax.experimental import pallas as pl
from jax.experimental.pallas import tpu as pltpu
from jax.sharding import Mesh
from jax.sharding import PartitionSpec as P

HEADS = 8
LATENTS = 4
HOPS = 3
E = 512
HEAD = E // HEADS
NLAT = 64
NLON = 512
LEV = 8
SEC = NLON // LEV
LEV_DEV = 5
GROUP = 32
FEATS = LATENTS * E // LEV
COMBOS = FEATS // HEAD
ROWS = FEATS + 16
RING = (0, 2, 4, 6, 7, 5, 3, 1)
CHUNKS = 2
CELLS = NLON // CHUNKS
F32 = jnp.float32
BF16 = jnp.bfloat16
NT = (((1,), (1,)), ((), ()))
VMEM_LIMIT = 8 * 1024 * 1024
LEVEL_LIMIT = 24 * 1024 * 1024


def pieces(x):
    high = x.astype(BF16).astype(F32)
    rest = x - high
    mid = rest.astype(BF16).astype(F32)
    return high, mid, rest - mid


def stat_rows(lse, partner):
    high, mid, low = pieces(lse)
    empty = jnp.zeros((16 - 3 * COMBOS - 1, lse.shape[1]), F32)
    return jnp.concatenate([high, mid, low, partner, empty], axis=0).astype(BF16)


def block_of(lev):
    return (lev + lax.axis_index("half") * (LEV // 2)) % LEV


def ring_place(lev):
    return jnp.where(lev % 2 == 0, lev // 2, (2 * LEV - 1 - lev) // 2)


def grouped_softmax(scores, valid, lev):
    kept = [valid[lev * LEV_DEV + level] == 1 for level in range(LEV_DEV)]
    masked = [jnp.where(keep, score, -1e30) for keep, score in zip(kept, scores)]
    top = functools.reduce(jnp.maximum, masked)
    expo = [jnp.where(keep, jnp.exp(score - top), 0.0) for keep, score in zip(kept, masked)]
    total = functools.reduce(jnp.add, expo)
    return [part / total for part in expo], top + jnp.log(total)


def partner_row(partner, lev):
    lane = lax.broadcasted_iota(jnp.int32, (SEC, NLON), 1)
    same = lane % SEC == lax.broadcasted_iota(jnp.int32, (SEC, NLON), 0)
    same = jnp.logical_and(same, lane // SEC == lev)
    local = jnp.broadcast_to((partner[...] % SEC).astype(F32), (8, SEC)).astype(BF16)
    spread = jnp.where(same, 1.0, 0.0).astype(BF16)
    return jnp.dot(local, spread, preferred_element_type=F32)[0:1]


def head_rows(query, latent_rows):
    width = query.shape[1]
    lane_head = lax.broadcasted_iota(jnp.int32, (HEADS, width), 1) // HEAD
    own_head = lane_head == lax.broadcasted_iota(jnp.int32, (HEADS, width), 0)
    rows = [jnp.where(own_head, row, 0.0) for row in latent_rows]
    return jnp.concatenate(rows, axis=0).astype(BF16)


def score_of(spread, block, key_weight):
    keys = jnp.dot(block, key_weight[...], preferred_element_type=F32).astype(BF16)
    score = lax.dot_general(spread, keys, NT, preferred_element_type=F32)
    return score * (1.0 / math.sqrt(HEAD))


def first_kernel(
    valid_at, query_at, key_at, value_at, tokens_at, partner_at,
    first, other, second, values, weights, stats,
    valid, query, key_weight, value_weight, tokens, partner, sems,
):
    lev = lax.axis_index("lev")
    copies = [
        pltpu.make_async_copy(key_at, key_weight, sems.at[0]),
        pltpu.make_async_copy(value_at, value_weight, sems.at[1]),
        pltpu.make_async_copy(query_at, query, sems.at[2]),
        pltpu.make_async_copy(valid_at, valid, sems.at[3]),
        pltpu.make_async_copy(partner_at, partner, sems.at[4]),
    ]
    fetches = [
        pltpu.make_async_copy(tokens_at.at[level], tokens.at[level], sems.at[5 + level])
        for level in range(LEV_DEV)
    ]
    for copy in copies + fetches:
        copy.start()
    for copy in copies:
        copy.wait()
    rows = query[...].astype(F32)
    spread = head_rows(query, [rows[k : k + 1] for k in range(LATENTS)])
    value_t = value_weight[...].astype(F32).T.astype(BF16)
    scores = []
    for level in range(LEV_DEV):
        fetches[level].wait()
        here = tokens[level]
        scores.append(score_of(spread, here, key_weight))
        value = lax.dot_general(value_t, here, NT, preferred_element_type=F32)
        values[level] = value.astype(BF16).astype(F32)
    shares, lse = grouped_softmax(scores, valid, lev)
    for level in range(LEV_DEV):
        weights[level] = shares[level]
    across = partner_row(partner, lev)
    for block in range(LEV):
        stats[block] = stat_rows(lse[block * COMBOS : (block + 1) * COMBOS], across)

    for ahead, outs in ((LEV // 2, (first, other)), (LEV // 2 + 1, (second,))):
        place = (ring_place(lev) + ahead) % LEV
        block = block_of(jnp.where(place < LEV // 2, 2 * place, 2 * LEV - 1 - 2 * place))
        for place in range(COMBOS):
            head = pl.multiple_of((block % 2 * COMBOS + place) * HEAD, HEAD)
            row = pl.ds(block * COMBOS + place, 1)
            terms = [
                weights[level, row, :] * values[level, pl.ds(head, HEAD), :]
                for level in range(LEV_DEV)
            ]
            summed = functools.reduce(jnp.add, terms).astype(BF16)
            width = NLON // len(outs)
            for chunk, out in enumerate(outs):
                lanes = slice(chunk * width, (chunk + 1) * width)
                out[pl.ds(place * HEAD, HEAD), :] = summed[:, lanes]
        for chunk, out in enumerate(outs):
            out[pl.ds(FEATS, 16), :] = stats[block, :, pl.ds(chunk * width, width)]


def first_block(*args):
    hbm = pl.BlockSpec(memory_space=pltpu.HBM)
    vmem = pl.BlockSpec(memory_space=pltpu.VMEM)
    return pl.pallas_call(
        first_kernel,
        out_shape=(
            jax.ShapeDtypeStruct((ROWS, CELLS), BF16),
            jax.ShapeDtypeStruct((ROWS, CELLS), BF16),
            jax.ShapeDtypeStruct((ROWS, NLON), BF16),
            jax.ShapeDtypeStruct((LEV_DEV, E, NLON), F32),
            jax.ShapeDtypeStruct((LEV_DEV, LATENTS * HEADS, NLON), F32),
            jax.ShapeDtypeStruct((LEV, 16, NLON), BF16),
        ),
        in_specs=[hbm] * len(args),
        out_specs=(vmem,) * 6,
        scratch_shapes=[
            pltpu.SMEM((LEV * LEV_DEV,), jnp.int32),
            pltpu.VMEM((LATENTS, E), BF16),
            pltpu.VMEM((E, E), BF16),
            pltpu.VMEM((E, E), BF16),
            pltpu.VMEM((LEV_DEV, NLON, E), BF16),
            pltpu.VMEM((1, SEC), jnp.int32),
            pltpu.SemaphoreType.DMA((5 + LEV_DEV,)),
        ],
        compiler_params=pltpu.CompilerParams(vmem_limit_bytes=LEVEL_LIMIT),
        name="first_block",
    )(*[pltpu.with_memory_space_constraint(arg, pltpu.HBM) for arg in args])


def ring_slot(ahead):
    slot = jnp.where(ahead <= LEV // 2, LEV // 2 - ahead, ahead - 1)
    return jnp.where(ahead == 0, LEV - 1, slot)


def blocks_kernel(values, weights, stats, own):
    here = ring_place(lax.axis_index("lev"))
    slots = [
        ring_slot((ring_place(block_of(block)) + LEV - here) % LEV) for block in range(LEV)
    ]
    for head in range(HEADS):
        for lane in range(0, NLON, 128):
            lanes = pl.ds(lane, 128)
            terms = [
                values[level, pl.ds(head * HEAD, HEAD), lanes] for level in range(LEV_DEV)
            ]
            for latent in range(LATENTS):
                row = pl.ds(latent * HEADS + head, 1)
                summed = weights[0, row, lanes] * terms[0]
                for level in range(1, LEV_DEV):
                    summed = summed + weights[level, row, lanes] * terms[level]
                block, place = divmod(latent * HEADS + head, COMBOS)
                own[slots[block], pl.ds(place * HEAD, HEAD), lanes] = summed.astype(BF16)
    for block in range(LEV):
        own[slots[block], pl.ds(FEATS, 16), :] = stats[block]


def merged(*messages):
    stats = [message[pl.ds(FEATS, 16), :].astype(F32) for message in messages]
    n = COMBOS
    lses = [rows[0:n] + rows[n : 2 * n] + rows[2 * n : 3 * n] for rows in stats]
    best = functools.reduce(jnp.maximum, lses)
    grown = [jnp.exp(lse - best) for lse in lses]
    total = functools.reduce(jnp.add, grown)
    shares = [part / total for part in grown]
    partner = functools.reduce(jnp.add, [rows[3 * n : 3 * n + 1] for rows in stats])
    blocks = []
    for place in range(COMBOS):
        rows = pl.ds(place * HEAD, HEAD)
        terms = [
            share[place : place + 1] * message[rows, :].astype(F32)
            for share, message in zip(shares, messages)
        ]
        blocks.append(functools.reduce(jnp.add, terms))
    return blocks, best + jnp.log(total), partner


def lanes_of(chunk):
    return pl.ds(chunk * CELLS, CELLS)


def hop_kernel(slot, came_lanes, lanes, came, own, out):
    blocks, lse, partner = merged(came.at[:, came_lanes], own.at[slot, :, lanes])
    for place in range(COMBOS):
        out[pl.ds(place * HEAD, HEAD), :] = blocks[place].astype(BF16)
    out[pl.ds(FEATS, 16), :] = stat_rows(lse, partner)


def last_kernel(*refs):
    forward, (backward, own, out, across) = refs[:CHUNKS], refs[CHUNKS:]
    for chunk in range(CHUNKS):
        lanes = lanes_of(chunk)
        blocks, _, partner = merged(
            forward[chunk], backward.at[:, lanes], own.at[LEV - 1, :, lanes]
        )
        for place in range(COMBOS):
            out[pl.ds(place * HEAD, HEAD), lanes] = blocks[place].astype(BF16)
        across[:, lanes] = jnp.broadcast_to(partner, (8, CELLS))


def vmem_call(kernel, out_shape, name, *args, scratch=()):
    vmem = pl.BlockSpec(memory_space=pltpu.VMEM)
    return pl.pallas_call(
        kernel,
        out_shape=out_shape,
        in_specs=[vmem] * len(args),
        out_specs=jax.tree.map(lambda _: vmem, out_shape),
        scratch_shapes=scratch,
        compiler_params=pltpu.CompilerParams(vmem_limit_bytes=VMEM_LIMIT),
        name=name,
    )(*args)


def pole_matrix(across):
    lane = lax.broadcasted_iota(jnp.int32, (1, NLON), 1)
    sector = (lane // SEC + LEV // 2) % LEV
    source = sector * SEC + across[0:1, :].astype(jnp.int32)
    place = lax.broadcasted_iota(jnp.int32, (NLON, NLON), 0)
    return jnp.where(place == source, 1.0, 0.0).astype(BF16)


def area_of(row):
    return math.cos(math.pi * (row + 0.5) / NLAT - math.pi / 2)


def coefficients(row):
    area, polar, inner = area_of(row), area_of(max(row - 1, 0)), area_of(row + 1)
    denom = 3.0 * area + polar + inner
    return area / denom, polar / denom, inner / denom


def edge_kernel(rows, out):
    out[...] = rows[pl.ds((GROUP - HOPS) * (1 - lax.axis_index("half")), HOPS)]


def diffuse_rows(start, low, high, pole, one, two, store):
    readers = (start, lambda row: one[row], lambda row: two[row])
    for step in range(HOPS):
        read = readers[step]
        reach = HOPS - 1 - step
        first = 0 if pole is not None else low - reach
        here = read(first)
        if pole is None:
            before = read(first - 1)
        else:
            top, mid, _ = pieces(here)
            both = jnp.concatenate([top, mid], axis=0).astype(BF16)
            turned = jnp.dot(both, pole, preferred_element_type=F32)
            before = turned[0:8] + turned[8:16]
        for row in range(first, high + reach):
            after = read(row + 1)
            area, polar, inner = coefficients(row)
            beside = pltpu.roll(here, 1, 1) + pltpu.roll(here, NLON - 1, 1)
            state = area * (here + beside) + polar * before + inner * after
            if step == 0:
                one[row] = state
            elif step == 1:
                two[row] = state
            else:
                total = start(row) + one[row] + here + state
                store(row, total * (1.0 / (HOPS + 1.0)))
            before, here = here, after


def inner_kernel(rows, across, out, raw, one, two):
    south = lax.axis_index("half")
    raw[...] = rows[...].astype(F32)

    def place(row):
        return row + south * (GROUP - 1 - 2 * row)

    def store(row, value):
        out[place(row)] = value.astype(BF16)

    pole = pole_matrix(across)
    diffuse_rows(lambda row: raw[place(row)], 0, GROUP - HOPS, pole, one, two, store)


def outer_kernel(rows, halo, inner, out, raw, edge, one, two):
    south = lax.axis_index("half")
    raw[...] = rows[...].astype(F32)
    edge[...] = halo[...].astype(F32)
    out[...] = inner[...]

    def place(row):
        return row + south * (GROUP - 1 - 2 * row)

    def start(row):
        if row < GROUP:
            return raw[place(row)]
        k = row - GROUP
        return edge[k + south * (HOPS - 1 - 2 * k)]

    def store(row, value):
        out[place(row)] = value.astype(BF16)

    diffuse_rows(start, GROUP - HOPS, GROUP, None, one, two, store)


def state_rows(count):
    return pltpu.VMEM((count, 8, NLON), F32)


def project_kernel(parts, weight, out):
    low = jnp.concatenate([parts[block_of(2 * k)] for k in range(LATENTS)], axis=0)
    high = jnp.concatenate([parts[block_of(2 * k + 1)] for k in range(LATENTS)], axis=0)
    summed = jnp.dot(low, weight[0:FEATS], preferred_element_type=F32)
    summed += jnp.dot(high, weight[FEATS:E], preferred_element_type=F32)
    for latent in range(LATENTS):
        rows = slice(latent * SEC, (latent + 1) * SEC)
        out[0, :, pl.ds(latent * E, E)] = summed[rows].astype(BF16)


def body(
    level_tokens, latent_queries, key_weight, value_weight, out_weight, level_valid, pole_partner
):
    tokens = jnp.transpose(level_tokens[0], (1, 0, 2))
    ring = [(RING[i], RING[(i + 1) % LEV]) for i in range(LEV)]
    args = (
        level_valid, latent_queries, key_weight, value_weight, tokens, pole_partner[None]
    )
    *forward, backward, values, weights, stats = first_block(*args)
    forward = [lax.ppermute(message, "lev", ring) for message in forward]
    whole = jax.ShapeDtypeStruct((ROWS, NLON), BF16)
    part = jax.ShapeDtypeStruct((ROWS, CELLS), BF16)
    shape = jax.ShapeDtypeStruct((LEV, *whole.shape), BF16)
    own = vmem_call(blocks_kernel, shape, "all_blocks", values, weights, stats)
    back = [(there, here) for here, there in ring]
    everything = slice(None)
    for step in range(1, LEV // 2):
        backward = lax.ppermute(backward, "lev", back)
        for chunk in range(CHUNKS):
            lanes = lanes_of(chunk)
            merge = functools.partial(hop_kernel, step, everything, lanes)
            going = vmem_call(merge, part, "hop", forward[chunk], own)
            forward[chunk] = lax.ppermute(going, "lev", ring)
        if step < LEV // 2 - 1:
            merge = functools.partial(hop_kernel, LEV // 2 + step, everything, everything)
            backward = vmem_call(merge, whole, "hop", backward, own)
    pooled, across = vmem_call(
        last_kernel,
        (
            jax.ShapeDtypeStruct((FEATS, NLON), BF16),
            jax.ShapeDtypeStruct((8, NLON), F32),
        ),
        "last_hop",
        *forward,
        backward,
        own,
    )

    rows = pooled.reshape(GROUP, FEATS // GROUP, NLON)
    rows = lax.all_to_all(rows, "row", split_axis=0, concat_axis=0, tiled=True)
    shape = jax.ShapeDtypeStruct((HOPS, *rows.shape[1:]), BF16)
    edge = vmem_call(edge_kernel, shape, "edge", rows)
    turned = [(lev, LEV + (lev + LEV // 2) % LEV) for lev in range(LEV)]
    turned += [(there, here) for here, there in turned]
    halo = lax.ppermute(edge, ("half", "lev"), turned)
    shape = jax.ShapeDtypeStruct(rows.shape, BF16)
    states = [state_rows(GROUP), state_rows(GROUP + HOPS), state_rows(GROUP + HOPS)]
    mean = vmem_call(inner_kernel, shape, "diffuse_inner", rows, across, scratch=states)
    states.insert(1, state_rows(HOPS))
    mean = vmem_call(outer_kernel, shape, "diffuse_outer", rows, halo, mean, scratch=states)
    mean = lax.all_to_all(mean, "row", split_axis=0, concat_axis=0, tiled=True)
    sectors = mean.reshape(FEATS, NLON).T.reshape(LEV, SEC, FEATS)
    parts = lax.all_to_all(sectors, "lev", split_axis=0, concat_axis=0, tiled=True)
    shape = jax.ShapeDtypeStruct((1, SEC, LATENTS * E), BF16)
    return vmem_call(project_kernel, shape, "project", parts, out_weight)


def solution(mesh):
    halves = mesh.shape["lat"] // GROUP
    devices = mesh.devices.reshape(halves, GROUP, mesh.shape["lev"])
    mesh = Mesh(devices, ("half", "row", "lev"))
    lat = ("half", "row")
    in_specs = (P(lat, None, "lev", None), P(), P(), P(), P(), P(), P("lev"))
    out_specs = P(lat, "lev", None)
    return jax.shard_map(body, mesh=mesh, in_specs=in_specs, out_specs=out_specs, check_vma=False)
```

```python
import functools
import math

import jax
import jax.numpy as jnp
from jax import lax
from jax.experimental import pallas as pl
from jax.experimental.pallas import tpu as pltpu
from jax.sharding import Mesh
from jax.sharding import PartitionSpec as P

HEADS = 8
LATENTS = 4
HOPS = 3
E = 512
HEAD = E // HEADS
NLAT = 64
NLON = 512
LEV = 8
SEC = NLON // LEV
LEV_DEV = 5
GROUP = 32
FEATS = LATENTS * E // LEV
COMBOS = FEATS // HEAD
ROWS = FEATS + 16
RING = (0, 2, 4, 6, 7, 5, 3, 1)
CHUNKS = 2
CELLS = NLON // CHUNKS
F32 = jnp.float32
BF16 = jnp.bfloat16
NT = (((1,), (1,)), ((), ()))
VMEM_LIMIT = 8 * 1024 * 1024
LEVEL_LIMIT = 24 * 1024 * 1024


def pieces(x):
    high = x.astype(BF16).astype(F32)
    rest = x - high
    mid = rest.astype(BF16).astype(F32)
    return high, mid, rest - mid


def stat_rows(lse, partner):
    high, mid, low = pieces(lse)
    empty = jnp.zeros((16 - 3 * COMBOS - 1, lse.shape[1]), F32)
    return jnp.concatenate([high, mid, low, partner, empty], axis=0).astype(BF16)


def block_of(lev):
    return (lev + lax.axis_index("half") * (LEV // 2)) % LEV


def ring_place(lev):
    return jnp.where(lev % 2 == 0, lev // 2, (2 * LEV - 1 - lev) // 2)


def grouped_softmax(scores, valid, lev):
    kept = [valid[lev * LEV_DEV + level] == 1 for level in range(LEV_DEV)]
    masked = [jnp.where(keep, score, -1e30) for keep, score in zip(kept, scores)]
    top = functools.reduce(jnp.maximum, masked)
    expo = [jnp.where(keep, jnp.exp(score - top), 0.0) for keep, score in zip(kept, masked)]
    total = functools.reduce(jnp.add, expo)
    return [part / total for part in expo], top + jnp.log(total)


def partner_row(partner, lev):
    lane = lax.broadcasted_iota(jnp.int32, (SEC, NLON), 1)
    same = lane % SEC == lax.broadcasted_iota(jnp.int32, (SEC, NLON), 0)
    same = jnp.logical_and(same, lane // SEC == lev)
    local = jnp.broadcast_to((partner[...] % SEC).astype(F32), (8, SEC)).astype(BF16)
    spread = jnp.where(same, 1.0, 0.0).astype(BF16)
    return jnp.dot(local, spread, preferred_element_type=F32)[0:1]


def head_rows(query, latent_rows):
    width = query.shape[1]
    lane_head = lax.broadcasted_iota(jnp.int32, (HEADS, width), 1) // HEAD
    own_head = lane_head == lax.broadcasted_iota(jnp.int32, (HEADS, width), 0)
    rows = [jnp.where(own_head, row, 0.0) for row in latent_rows]
    return jnp.concatenate(rows, axis=0).astype(BF16)


def score_of(spread, block, key_weight):
    keys = jnp.dot(block, key_weight[...], preferred_element_type=F32).astype(BF16)
    score = lax.dot_general(spread, keys, NT, preferred_element_type=F32)
    return score * (1.0 / math.sqrt(HEAD))


def first_kernel(
    valid_at, query_at, key_at, value_at, tokens_at, partner_at,
    first, other, second, values, weights, stats,
    valid, query, key_weight, value_weight, tokens, partner, sems,
):
    lev = lax.axis_index("lev")
    copies = [
        pltpu.make_async_copy(key_at, key_weight, sems.at[0]),
        pltpu.make_async_copy(value_at, value_weight, sems.at[1]),
        pltpu.make_async_copy(query_at, query, sems.at[2]),
        pltpu.make_async_copy(valid_at, valid, sems.at[3]),
        pltpu.make_async_copy(partner_at, partner, sems.at[4]),
    ]
    fetches = [
        pltpu.make_async_copy(tokens_at.at[level], tokens.at[level], sems.at[5 + level])
        for level in range(LEV_DEV)
    ]
    for copy in copies + fetches:
        copy.start()
    for copy in copies:
        copy.wait()
    rows = query[...].astype(F32)
    spread = head_rows(query, [rows[k : k + 1] for k in range(LATENTS)])
    value_t = value_weight[...].astype(F32).T.astype(BF16)
    scores = []
    for level in range(LEV_DEV):
        fetches[level].wait()
        here = tokens[level]
        scores.append(score_of(spread, here, key_weight))
        value = lax.dot_general(value_t, here, NT, preferred_element_type=F32)
        values[level] = value.astype(BF16).astype(F32)
    shares, lse = grouped_softmax(scores, valid, lev)
    for level in range(LEV_DEV):
        weights[level] = shares[level]
    across = partner_row(partner, lev)
    for block in range(LEV):
        stats[block] = stat_rows(lse[block * COMBOS : (block + 1) * COMBOS], across)

    for ahead, outs in ((LEV // 2, (first, other)), (LEV // 2 + 1, (second,))):
        place = (ring_place(lev) + ahead) % LEV
        block = block_of(jnp.where(place < LEV // 2, 2 * place, 2 * LEV - 1 - 2 * place))
        for place in range(COMBOS):
            head = pl.multiple_of((block % 2 * COMBOS + place) * HEAD, HEAD)
            row = pl.ds(block * COMBOS + place, 1)
            terms = [
                weights[level, row, :] * values[level, pl.ds(head, HEAD), :]
                for level in range(LEV_DEV)
            ]
            summed = functools.reduce(jnp.add, terms).astype(BF16)
            width = NLON // len(outs)
            for chunk, out in enumerate(outs):
                lanes = slice(chunk * width, (chunk + 1) * width)
                out[pl.ds(place * HEAD, HEAD), :] = summed[:, lanes]
        for chunk, out in enumerate(outs):
            out[pl.ds(FEATS, 16), :] = stats[block, :, pl.ds(chunk * width, width)]


def first_block(*args):
    hbm = pl.BlockSpec(memory_space=pltpu.HBM)
    vmem = pl.BlockSpec(memory_space=pltpu.VMEM)
    return pl.pallas_call(
        first_kernel,
        out_shape=(
            jax.ShapeDtypeStruct((ROWS, CELLS), BF16),
            jax.ShapeDtypeStruct((ROWS, CELLS), BF16),
            jax.ShapeDtypeStruct((ROWS, NLON), BF16),
            jax.ShapeDtypeStruct((LEV_DEV, E, NLON), F32),
            jax.ShapeDtypeStruct((LEV_DEV, LATENTS * HEADS, NLON), F32),
            jax.ShapeDtypeStruct((LEV, 16, NLON), BF16),
        ),
        in_specs=[hbm] * len(args),
        out_specs=(vmem,) * 6,
        scratch_shapes=[
            pltpu.SMEM((LEV * LEV_DEV,), jnp.int32),
            pltpu.VMEM((LATENTS, E), BF16),
            pltpu.VMEM((E, E), BF16),
            pltpu.VMEM((E, E), BF16),
            pltpu.VMEM((LEV_DEV, NLON, E), BF16),
            pltpu.VMEM((1, SEC), jnp.int32),
            pltpu.SemaphoreType.DMA((5 + LEV_DEV,)),
        ],
        compiler_params=pltpu.CompilerParams(vmem_limit_bytes=LEVEL_LIMIT),
        name="first_block",
    )(*[pltpu.with_memory_space_constraint(arg, pltpu.HBM) for arg in args])


def ring_slot(ahead):
    slot = jnp.where(ahead <= LEV // 2, LEV // 2 - ahead, ahead - 1)
    return jnp.where(ahead == 0, LEV - 1, slot)


def blocks_kernel(values, weights, stats, own):
    here = ring_place(lax.axis_index("lev"))
    slots = [
        ring_slot((ring_place(block_of(block)) + LEV - here) % LEV) for block in range(LEV)
    ]
    for head in range(HEADS):
        for lane in range(0, NLON, 128):
            lanes = pl.ds(lane, 128)
            terms = [
                values[level, pl.ds(head * HEAD, HEAD), lanes] for level in range(LEV_DEV)
            ]
            for latent in range(LATENTS):
                row = pl.ds(latent * HEADS + head, 1)
                summed = weights[0, row, lanes] * terms[0]
                for level in range(1, LEV_DEV):
                    summed = summed + weights[level, row, lanes] * terms[level]
                block, place = divmod(latent * HEADS + head, COMBOS)
                own[slots[block], pl.ds(place * HEAD, HEAD), lanes] = summed.astype(BF16)
    for block in range(LEV):
        own[slots[block], pl.ds(FEATS, 16), :] = stats[block]


def merged(*messages):
    stats = [message[pl.ds(FEATS, 16), :].astype(F32) for message in messages]
    n = COMBOS
    lses = [rows[0:n] + rows[n : 2 * n] + rows[2 * n : 3 * n] for rows in stats]
    best = functools.reduce(jnp.maximum, lses)
    grown = [jnp.exp(lse - best) for lse in lses]
    total = functools.reduce(jnp.add, grown)
    shares = [part / total for part in grown]
    partner = functools.reduce(jnp.add, [rows[3 * n : 3 * n + 1] for rows in stats])
    blocks = []
    for place in range(COMBOS):
        rows = pl.ds(place * HEAD, HEAD)
        terms = [
            share[place : place + 1] * message[rows, :].astype(F32)
            for share, message in zip(shares, messages)
        ]
        blocks.append(functools.reduce(jnp.add, terms))
    return blocks, best + jnp.log(total), partner


def lanes_of(chunk):
    return pl.ds(chunk * CELLS, CELLS)


def hop_kernel(slot, came_lanes, lanes, came, own, *refs):
    out = refs[-1]
    blocks, lse, partner = merged(came.at[:, came_lanes], own.at[slot, :, lanes])
    for place in range(COMBOS):
        out[pl.ds(place * HEAD, HEAD), :] = blocks[place].astype(BF16)
    out[pl.ds(FEATS, 16), :] = stat_rows(lse, partner)


def last_kernel(*refs):
    forward, (backward, own, out, across) = refs[:CHUNKS], refs[CHUNKS:]
    for chunk in range(CHUNKS):
        lanes = lanes_of(chunk)
        blocks, _, partner = merged(
            forward[chunk], backward.at[:, lanes], own.at[LEV - 1, :, lanes]
        )
        for place in range(COMBOS):
            out[pl.ds(place * HEAD, HEAD), lanes] = blocks[place].astype(BF16)
        across[:, lanes] = jnp.broadcast_to(partner, (8, CELLS))


def vmem_call(kernel, out_shape, name, *args, scratch=()):
    vmem = pl.BlockSpec(memory_space=pltpu.VMEM)
    return pl.pallas_call(
        kernel,
        out_shape=out_shape,
        in_specs=[vmem] * len(args),
        out_specs=jax.tree.map(lambda _: vmem, out_shape),
        scratch_shapes=scratch,
        compiler_params=pltpu.CompilerParams(vmem_limit_bytes=VMEM_LIMIT),
        name=name,
    )(*args)


def pole_matrix(across):
    lane = lax.broadcasted_iota(jnp.int32, (1, NLON), 1)
    sector = (lane // SEC + LEV // 2) % LEV
    source = sector * SEC + across[0:1, :].astype(jnp.int32)
    place = lax.broadcasted_iota(jnp.int32, (NLON, NLON), 0)
    return jnp.where(place == source, 1.0, 0.0).astype(BF16)


def area_of(row):
    return math.cos(math.pi * (row + 0.5) / NLAT - math.pi / 2)


def coefficients(row):
    area, polar, inner = area_of(row), area_of(max(row - 1, 0)), area_of(row + 1)
    denom = 3.0 * area + polar + inner
    return area / denom, polar / denom, inner / denom


def edge_kernel(rows, out):
    out[...] = rows[pl.ds((GROUP - HOPS) * (1 - lax.axis_index("half")), HOPS)]


def diffuse_rows(start, low, high, pole, one, two, store):
    readers = (start, lambda row: one[row], lambda row: two[row])
    for step in range(HOPS):
        read = readers[step]
        reach = HOPS - 1 - step
        first = 0 if pole is not None else low - reach
        here = read(first)
        if pole is None:
            before = read(first - 1)
        else:
            top, mid, _ = pieces(here)
            both = jnp.concatenate([top, mid], axis=0).astype(BF16)
            turned = jnp.dot(both, pole, preferred_element_type=F32)
            before = turned[0:8] + turned[8:16]
        for row in range(first, high + reach):
            after = read(row + 1)
            area, polar, inner = coefficients(row)
            beside = pltpu.roll(here, 1, 1) + pltpu.roll(here, NLON - 1, 1)
            state = area * (here + beside) + polar * before + inner * after
            if step == 0:
                one[row] = state
            elif step == 1:
                two[row] = state
            else:
                total = start(row) + one[row] + here + state
                store(row, total * (1.0 / (HOPS + 1.0)))
            before, here = here, after


def inner_kernel(rows, across, out, raw, one, two):
    south = lax.axis_index("half")
    raw[...] = rows[...].astype(F32)

    def place(row):
        return row + south * (GROUP - 1 - 2 * row)

    def store(row, value):
        out[place(row)] = value.astype(BF16)

    pole = pole_matrix(across)
    diffuse_rows(lambda row: raw[place(row)], 0, GROUP - HOPS, pole, one, two, store)


def outer_kernel(rows, halo, inner, out, raw, edge, one, two):
    south = lax.axis_index("half")
    raw[...] = rows[...].astype(F32)
    edge[...] = halo[...].astype(F32)
    out[...] = inner[...]

    def place(row):
        return row + south * (GROUP - 1 - 2 * row)

    def start(row):
        if row < GROUP:
            return raw[place(row)]
        k = row - GROUP
        return edge[k + south * (HOPS - 1 - 2 * k)]

    def store(row, value):
        out[place(row)] = value.astype(BF16)

    diffuse_rows(start, GROUP - HOPS, GROUP, None, one, two, store)


def state_rows(count):
    return pltpu.VMEM((count, 8, NLON), F32)


def project_kernel(parts, weight, out):
    low = jnp.concatenate([parts[block_of(2 * k)] for k in range(LATENTS)], axis=0)
    high = jnp.concatenate([parts[block_of(2 * k + 1)] for k in range(LATENTS)], axis=0)
    summed = jnp.dot(low, weight[0:FEATS], preferred_element_type=F32)
    summed += jnp.dot(high, weight[FEATS:E], preferred_element_type=F32)
    for latent in range(LATENTS):
        rows = slice(latent * SEC, (latent + 1) * SEC)
        out[0, :, pl.ds(latent * E, E)] = summed[rows].astype(BF16)


def body(
    level_tokens, latent_queries, key_weight, value_weight, out_weight, level_valid, pole_partner
):
    tokens = jnp.transpose(level_tokens[0], (1, 0, 2))
    ring = [(RING[i], RING[(i + 1) % LEV]) for i in range(LEV)]
    args = (
        level_valid, latent_queries, key_weight, value_weight, tokens, pole_partner[None]
    )
    *forward, backward, values, weights, stats = first_block(*args)
    forward = [lax.ppermute(message, "lev", ring) for message in forward]
    whole = jax.ShapeDtypeStruct((ROWS, NLON), BF16)
    part = jax.ShapeDtypeStruct((ROWS, CELLS), BF16)
    shape = jax.ShapeDtypeStruct((LEV, *whole.shape), BF16)
    own = vmem_call(blocks_kernel, shape, "all_blocks", values, weights, stats)
    back = [(there, here) for here, there in ring]
    everything = slice(None)
    for step in range(1, LEV // 2):
        backward = lax.ppermute(backward, "lev", back)
        for chunk in range(CHUNKS):
            lanes = lanes_of(chunk)
            merge = functools.partial(hop_kernel, step, everything, lanes)
            going = vmem_call(merge, part, "hop", forward[chunk], own)
            forward[chunk] = lax.ppermute(going, "lev", ring)
        if step < LEV // 2 - 1:
            merge = functools.partial(hop_kernel, LEV // 2 + step, everything, everything)
            backward = vmem_call(merge, whole, "hop", backward, own, going)
    pooled, across = vmem_call(
        last_kernel,
        (
            jax.ShapeDtypeStruct((FEATS, NLON), BF16),
            jax.ShapeDtypeStruct((8, NLON), F32),
        ),
        "last_hop",
        *forward,
        backward,
        own,
    )

    rows = pooled.reshape(GROUP, FEATS // GROUP, NLON)
    rows = lax.all_to_all(rows, "row", split_axis=0, concat_axis=0, tiled=True)
    shape = jax.ShapeDtypeStruct((HOPS, *rows.shape[1:]), BF16)
    edge = vmem_call(edge_kernel, shape, "edge", rows)
    turned = [(lev, LEV + (lev + LEV // 2) % LEV) for lev in range(LEV)]
    turned += [(there, here) for here, there in turned]
    halo = lax.ppermute(edge, ("half", "lev"), turned)
    shape = jax.ShapeDtypeStruct(rows.shape, BF16)
    states = [state_rows(GROUP), state_rows(GROUP + HOPS), state_rows(GROUP + HOPS)]
    mean = vmem_call(inner_kernel, shape, "diffuse_inner", rows, across, scratch=states)
    states.insert(1, state_rows(HOPS))
    mean = vmem_call(outer_kernel, shape, "diffuse_outer", rows, halo, mean, scratch=states)
    mean = lax.all_to_all(mean, "row", split_axis=0, concat_axis=0, tiled=True)
    sectors = mean.reshape(FEATS, NLON).T.reshape(LEV, SEC, FEATS)
    parts = lax.all_to_all(sectors, "lev", split_axis=0, concat_axis=0, tiled=True)
    shape = jax.ShapeDtypeStruct((1, SEC, LATENTS * E), BF16)
    return vmem_call(project_kernel, shape, "project", parts, out_weight)


def solution(mesh):
    halves = mesh.shape["lat"] // GROUP
    devices = mesh.devices.reshape(halves, GROUP, mesh.shape["lev"])
    mesh = Mesh(devices, ("half", "row", "lev"))
    lat = ("half", "row")
    in_specs = (P(lat, None, "lev", None), P(), P(), P(), P(), P(), P("lev"))
    out_specs = P(lat, "lev", None)
    return jax.shard_map(body, mesh=mesh, in_specs=in_specs, out_specs=out_specs, check_vma=False)
```
